512 devices in a mesh: uly: 4 (over z_lo), row: 8 (over x, core), col: 16 (over z_hi, y).
Axes of the slice: x: 4, y: 4, z: 16 (z_hi: 4, z_lo: 4; z = z_hi * 4 + z_lo), core: 2. Of those that a mesh axis runs over, the one named last changes fastest.
Arguments:
- queries: bfloat16 [1024, 4096], P(('row', 'col', 'uly')), may hold values from -8 to 8
- keys: bfloat16 [65536, 1024], P(('col', 'row', 'uly')), may hold values from -8 to 8
- values: bfloat16 [65536, 1024], P(('col', 'row', 'uly')), may hold values from -6 to 6
- window_blocks: int32 [16], replicated, may hold values from 0 to 1023, as said below
Outputs:
- attended: bfloat16 [1024, 4096], P(('row', 'col', 'uly'))
The draws below stay inside these ranges and needn't reach their ends.
Inputs may be any that keep to these rules, and one draw needn't show every extreme that they name: `window_blocks`: distinct blocks of 64 positions; entries 2r and 2r + 1 are the (r + 1)-th earliest and the (r + 1)-th latest of the 16 blocks; the first and the last block of the sequence are always among them.
All inputs are finite; a program needn't handle non-finite values.
Results may differ from the reference program's by a relative error of at most 0.015.
Values may be sent and summed in bfloat16 or wider, within the bound.
A program may use at most 64 MiB of HBM per device.

```python
import math
import jax
import jax.numpy as jnp
import numpy as np
from jax import lax

QUERY_HEAD_COUNT = 32
KEY_VALUE_HEADS = 8
HEAD_SIZE = 128
BLOCK_QUERY_ROWS = 64
SEQUENCE_TOKENS = 65536
WINDOW_BLOCKS_N = 16
QROWS = 1024


def draw_queries(key, part):
    key = jax.random.fold_in(key, 5)
    return (1.6 * jax.random.truncated_normal(key, -5.0, 5.0, (QROWS, QUERY_HEAD_COUNT * HEAD_SIZE), jnp.float32)).astype(jnp.bfloat16)


def draw_keys(key, part):
    key = jax.random.fold_in(key, 9)
    return (1.6 * jax.random.truncated_normal(key, -5.0, 5.0, (SEQUENCE_TOKENS, KEY_VALUE_HEADS * HEAD_SIZE), jnp.float32)).astype(jnp.bfloat16)


def draw_window_blocks(key, part):
    key = jax.random.fold_in(key, 13)
    block_count = SEQUENCE_TOKENS // BLOCK_QUERY_ROWS
    inner = jax.random.permutation(key, block_count - 2)[:WINDOW_BLOCKS_N - 2].astype(jnp.int32) + 1
    ends = jnp.array([0, block_count - 1], jnp.int32)
    picked = jnp.sort(jnp.concatenate([ends, inner]))
    order = np.array([j // 2 if j % 2 == 0 else WINDOW_BLOCKS_N - 1 - j // 2 for j in range(WINDOW_BLOCKS_N)], np.int32)
    return picked[order].astype(jnp.int32)


def steps_of(rng, shape, cuts, smallest, largest):
    loudness, own = 1.0, jax.random.fold_in(rng, 6)
    for axis_at, shards_of in cuts:
        heights = jnp.exp(jax.random.uniform(jax.random.fold_in(own, axis_at), (shards_of,), jnp.float32, smallest / len(cuts), largest / len(cuts)))
        loudness = loudness * jnp.repeat(heights, shape[axis_at] // shards_of).reshape([-1 if axis == axis_at else 1 for axis in range(len(shape))])
    return loudness


def gaussian(key, shape, deviation, limit, cuts=(), held_as=jnp.bfloat16):
    values = deviation * jax.random.normal(key, shape, jnp.float32)
    if cuts:
        values = values * steps_of(key, shape, cuts, -0.22, 0.18)
    return jnp.clip(values, -limit, limit).astype(held_as)


def setup_inputs(seed: int = 0) -> dict:
    arg_keys = jax.random.split(jax.random.key(seed), 5)
    return {
        "queries": draw_queries(jax.random.fold_in(arg_keys[4], 71), 0),
        "keys": draw_keys(jax.random.fold_in(arg_keys[4], 71), 0),
        "values": gaussian(arg_keys[2], (SEQUENCE_TOKENS, KEY_VALUE_HEADS * HEAD_SIZE), 1.0, 6.0, ((0, 512),)),
        "window_blocks": draw_window_blocks(jax.random.fold_in(arg_keys[4], 71), 0),
    }


def reference(queries, keys, values, window_blocks):
    queries_per_group = QUERY_HEAD_COUNT // KEY_VALUE_HEADS
    score_scale = 1.0 / math.sqrt(HEAD_SIZE)
    row_ids = jnp.arange(QROWS, dtype=jnp.int32)
    query_pos = (window_blocks[row_ids // BLOCK_QUERY_ROWS] * BLOCK_QUERY_ROWS + row_ids % BLOCK_QUERY_ROWS).astype(jnp.int32)
    key_pos = jnp.arange(SEQUENCE_TOKENS, dtype=jnp.int32)
    query_block_tiles = queries.reshape(WINDOW_BLOCKS_N, BLOCK_QUERY_ROWS, KEY_VALUE_HEADS, queries_per_group, HEAD_SIZE)
    pos_tiles = query_pos.reshape(WINDOW_BLOCKS_N, BLOCK_QUERY_ROWS)

    def one_block(item_pair):
        query_tile, row_pos = item_pair
        visible = key_pos[None, :] <= row_pos[:, None]
        head_outputs = []
        for key_value_head in range(KEY_VALUE_HEADS):
            query_f32 = query_tile[:, key_value_head].astype(jnp.float32)
            key_f32 = keys[:, key_value_head * HEAD_SIZE:(key_value_head + 1) * HEAD_SIZE].astype(jnp.float32)
            value_f32 = values[:, key_value_head * HEAD_SIZE:(key_value_head + 1) * HEAD_SIZE].astype(jnp.float32)
            scores = jnp.einsum('qgd,kd->gqk', query_f32, key_f32, precision=lax.Precision.HIGHEST) * score_scale
            scores = jnp.where(visible[None], scores, -jnp.inf)
            row_top = lax.optimization_barrier(jnp.max(scores, axis=-1, keepdims=True))
            weights = jnp.where(visible[None], jnp.exp(scores - row_top), 0.0)
            totals = lax.optimization_barrier(jnp.sum(weights, axis=-1))
            weights_bf16 = lax.optimization_barrier(weights.astype(jnp.bfloat16)).astype(jnp.float32)
            attended = jnp.einsum('gqk,kd->qgd', weights_bf16, value_f32, precision=lax.Precision.HIGHEST)
            attended = attended / totals.T[:, :, None]
            head_outputs.append(attended.reshape(BLOCK_QUERY_ROWS, queries_per_group * HEAD_SIZE))
        return jnp.concatenate(head_outputs, axis=1).astype(jnp.bfloat16)
    return lax.map(one_block, (query_block_tiles, pos_tiles)).reshape(QROWS, QUERY_HEAD_COUNT * HEAD_SIZE)
```

```python
import math

import jax
import jax.numpy as jnp
from jax import lax
from jax.experimental import pallas as pl
from jax.experimental.pallas import tpu as pltpu
from jax.sharding import PartitionSpec as P

HEAD = 128
MESH = pl.DeviceIdType.MESH
SCALE = math.log2(math.e) / math.sqrt(HEAD)
HIDDEN = -1e30
F32, BF16 = jnp.float32, jnp.bfloat16


def expand(row):
    return jnp.transpose(jnp.broadcast_to(row, (HEAD, HEAD)))


def kernel(
    q_ref, k_ref, v_ref, wb_ref, out_ref,
    q_out, q_in, q_all, k_all, v_all, thr,
    o_all, l_all, o_in, l_in,
    p_out, lp_out, p_in, lp_in,
    z_out, lz_out, z_in, lz_in, f_out, f_in,
    q1s, q1r, ks, kr, vs, vr, own_sem,
    q2s, q2r, q3s, q3r, q4s, q4r,
    osn, orc, lsn, lrc, psn, prc, lpsn, lprc,
    zsn, zrc, lzsn, lzrc, fsn, frc,
):
    u = lax.axis_index("uly")
    row = lax.axis_index("row")
    col = lax.axis_index("col")
    x, core = row // 2, row % 2
    y = col % 4
    z = (col // 4) * 4 + u

    def dev(x_at, y_at, z_at, core_at):
        z_at = (z_at + 16) % 16
        return {
            "uly": z_at % 4,
            "row": (x_at % 4) * 2 + core_at,
            "col": (z_at // 4) * 4 + y_at % 4,
        }

    def remote(src, dst, send, recv, to):
        return pltpu.make_async_remote_copy(
            src_ref=src, dst_ref=dst, send_sem=send, recv_sem=recv,
            device_id=to, device_id_type=MESH,
        )

    d2 = 2 - 4 * core
    targets = [(z, 1 - core, 1)]
    targets += [(z + 1, c, 2 + core) for c in range(2)]
    targets += [(z - 1, c, 4 + core) for c in range(2)]
    targets += [(z + d2, c, 6 + core) for c in range(2)]
    sources = [(z, 1 - core), (z - 1, 0), (z - 1, 1), (z + 1, 0), (z + 1, 1), (z - 2, 0), (z + 2, 1)]
    peers = [dev(x, y, zt, c) for zt, c, _ in targets] + [dev(x, y, z - d2, core)]
    peers += [dev(x, y, z + 4 * i, core) for i in range(1, 4)]
    peers += [dev(x + i, y, z, core) for i in range(1, 4)]
    peers += [dev(x, y + i, z, core) for i in range(1, 4)]

    def group_of(zt, c):
        return 2 * ((zt + 16) % 4) + c

    my_group = group_of(z, core)

    v_all[:, :, HEAD:] = jnp.ones((8, HEAD, HEAD), BF16)
    l_all[...] = jnp.zeros_like(l_all)
    lp_out[...] = jnp.zeros_like(lp_out)
    lz_out[...] = jnp.zeros_like(lz_out)
    barrier = pltpu.get_barrier_semaphore()
    for peer in peers:
        pl.semaphore_signal(barrier, inc=1, device_id=peer, device_id_type=MESH)
    for h in range(32):
        q_out[h // 4, 2 * (h % 4):2 * (h % 4) + 2, :] = q_ref[:, h * HEAD:(h + 1) * HEAD].astype(F32)
    pl.semaphore_wait(barrier, len(peers))

    sends = []

    def go(copy):
        copy.start()
        sends.append(copy)

    for n, (zt, c, slot) in enumerate(targets):
        go(remote(q_out.at[group_of(zt, c)], q_in.at[slot], q1s.at[n], q1r.at[slot], dev(x, y, zt, c)))

    def features(ref, group):
        return ref.at[:, pl.ds(pl.multiple_of(group * HEAD, HEAD), HEAD)]

    for n, (zt, c, slot) in enumerate(targets):
        to, group = dev(x, y, zt, c), group_of(zt, c)
        go(remote(features(k_ref, group), k_all.at[slot], ks.at[n], kr.at[slot], to))
        go(remote(features(v_ref, group), v_all.at[slot, :, pl.ds(0, HEAD)], vs.at[n], vr.at[slot], to))
    own_k = pltpu.make_async_copy(features(k_ref, my_group), k_all.at[0], own_sem.at[0])
    own_v = pltpu.make_async_copy(features(v_ref, my_group), v_all.at[0, :, pl.ds(0, HEAD)], own_sem.at[1])
    own_k.start()
    own_v.start()

    me = dev(x, y, z, 1 - core)

    def arrived(ref, sem):
        remote(ref, ref, sem, sem, me).wait_recv()

    q_in[0] = q_out[my_group]
    for slot in range(1, 8):
        arrived(q_in.at[slot], q1r.at[slot])
    q_all[0, 0, 0:64, :] = q_in[...].reshape(64, HEAD).astype(BF16)

    def z_place(ref, r):
        return ref.at[r // 2, 0, pl.ds((r % 2) * 64, 64)]

    for i in range(1, 4):
        go(remote(z_place(q_all, 0), z_place(q_all, 4 - i), q2s.at[i], q2r.at[4 - i], dev(x, y, z + 4 * i, core)))

    blk = lax.broadcasted_iota(jnp.int32, (32, HEAD), 0)
    lane = lax.broadcasted_iota(jnp.int32, (32, HEAD), 1)
    half, step, sub = (blk >> 2) & 1, blk >> 3, blk & 3
    ys = (y + jnp.where(half == 0, step, sub)) & 3
    xs = (x + jnp.where(half == 0, sub, step)) & 3
    slot = (lane >> 3) & 7
    cs = jnp.where(slot == 0, core, jnp.where(slot == 1, 1 - core, slot & 1))
    dz = jnp.where(slot < 2, 0, jnp.where(slot < 4, -1, jnp.where(slot < 6, 1, jnp.where(slot == 6, -2, 2))))
    zs = (z + 4 * (2 * half + (lane >> 6)) + dz + 16) & 15
    which = 2 * (2 * xs + cs) + (zs >> 3)
    block_at = jnp.zeros((32, HEAD), jnp.int32)
    for i in range(16):
        block_at = jnp.where(which == i, wb_ref[i], block_at)
    pos = 64 * block_at + ((((zs >> 2) & 1) * 4 + ys) * 8 + (zs & 3) * 2 + (lane & 1))
    pos = pos.astype(F32)
    for b in range(32):
        thr[b] = expand(pos[b:b + 1, :])

    arrived(z_place(q_all, 1), q2r.at[1])
    for i in range(1, 4):
        go(remote(q_all.at[0, 0], q_all.at[0, 4 - i], q3s.at[0, i], q3r.at[0, 4 - i], dev(x + i, y, z, core)))
    arrived(z_place(q_all, 2), q2r.at[2])
    arrived(z_place(q_all, 3), q2r.at[3])
    for i in range(1, 4):
        go(remote(q_all.at[1, 0], q_all.at[1, 4 - i], q3s.at[1, i], q3r.at[1, 4 - i], dev(x, y + i, z, core)))
    for r in range(1, 4):
        arrived(q_all.at[0, r], q3r.at[0, r])
    for i in range(1, 4):
        go(remote(q_all.at[0], q_all.at[2 * (4 - i)], q4s.at[2 * i], q4r.at[2 * (4 - i)], dev(x, y + i, z, core)))
    for r in range(1, 4):
        arrived(q_all.at[1, r], q3r.at[1, r])
    for i in range(1, 4):
        go(remote(q_all.at[1], q_all.at[2 * (4 - i) + 1], q4s.at[2 * i + 1], q4r.at[2 * (4 - i) + 1], dev(x + i, y, z, core)))

    own_k.wait()
    own_v.wait()
    for slot in range(1, 8):
        arrived(k_all.at[slot], kr.at[slot])
        arrived(v_all.at[slot, :, pl.ds(0, HEAD)], vr.at[slot])

    lane_f = lax.broadcasted_iota(jnp.int32, (1, HEAD), 1).astype(F32)
    key_pos = []
    for zt, c in [(z, core)] + sources:
        zt = (zt + 16) % 16
        base = (zt // 4) * 16384 + y * 4096 + x * 1024 + c * 512 + (zt % 4) * 128
        key_pos.append(lane_f + base.astype(F32))
    eye = lax.broadcasted_iota(jnp.int32, (HEAD, HEAD), 0) == lax.broadcasted_iota(jnp.int32, (HEAD, HEAD), 1)

    def squeeze(wide):
        return jnp.sum(jnp.where(eye, wide, 0.0), axis=0, keepdims=True)

    def result_copies(k):
        t, half = k // 2, k % 2
        to = dev(x + t * half, y + t * (1 - half), z, core)
        there = 2 * (4 - t) + half
        return (
            remote(o_all.at[k], o_in.at[there], osn.at[k], orc.at[there], to),
            remote(l_all.at[k], l_in.at[there], lsn.at[k], lrc.at[there], to),
        )

    def chunk(k, carry):
        @pl.when(k >= 2)
        def _():
            arrived(q_all.at[k], q4r.at[k])

        for pair in range(2):
            q = q_all[k, 2 * pair:2 * pair + 2].reshape(256, HEAD)
            scores = lax.dot_general(
                q, k_all[...].reshape(1024, HEAD), (((1,), (1,)), ((), ())), preferred_element_type=F32
            )
            limit = thr[pl.ds(4 * k + 2 * pair, 2)].reshape(256, HEAD)
            parts = [
                jnp.where(key_pos[j] <= limit, scores[:, j * HEAD:(j + 1) * HEAD], HIDDEN) for j in range(8)
            ]
            top = parts[0]
            for part in parts[1:]:
                top = jnp.maximum(top, part)
            top = jnp.max(top, axis=1, keepdims=True) * SCALE
            weights = jnp.concatenate([jnp.exp2(part * SCALE - top).astype(BF16) for part in parts], axis=1)
            both = lax.dot_general(
                weights, v_all[...].reshape(1024, 2 * HEAD), (((1,), (0,)), ((), ())), preferred_element_type=F32
            )
            total = both[:, HEAD:]
            o_all[k, pl.ds(256 * pair, 256), :] = (both[:, :HEAD] / total).astype(BF16)
            level = top + jnp.log2(total)
            for b in range(2):
                l_all[k, 2 * pair + b:2 * pair + b + 1, :] = squeeze(level[b * HEAD:(b + 1) * HEAD])

        @pl.when(k >= 2)
        def _():
            for copy in result_copies(k):
                copy.start()

        return carry

    lax.fori_loop(0, 8, chunk, 0)

    def combine(levels, values):
        top = levels[0]
        for level in levels[1:]:
            top = jnp.maximum(top, level)
        shares = [jnp.exp2(level - top) for level in levels]
        total = shares[0] + shares[1] + shares[2] + shares[3]
        inverse = 1.0 / total
        return top + jnp.log2(total), [share * inverse for share in shares]

    def weighted(shares, values):
        acc = expand(shares[0]) * values[0].astype(F32)
        for share, value in zip(shares[1:], values[1:]):
            acc = acc + expand(share) * value.astype(F32)
        return acc

    for half in range(2):
        for t in range(1, 4):
            arrived(o_in.at[2 * t + half], orc.at[2 * t + half])
            arrived(l_in.at[2 * t + half], lrc.at[2 * t + half])
        for b in (1, 2, 3, 0):
            levels = [l_all[half, b:b + 1, :]] + [l_in[2 * t + half, b:b + 1, :] for t in range(1, 4)]
            level, shares = combine(levels, None)
            rows = slice(b * HEAD, (b + 1) * HEAD)
            values = [o_all[half, rows, :]] + [o_in[2 * t + half, rows, :] for t in range(1, 4)]
            p_out[half, b] = weighted(shares, values).astype(BF16)
            lp_out[half, b, 0:1, :] = level
            if b:
                to = dev(x + b * (1 - half), y + b * half, z, core)
                go(remote(p_out.at[half, b], p_in.at[half, 4 - b], psn.at[half, b], prc.at[half, 4 - b], to))
                go(remote(lp_out.at[half, b], lp_in.at[half, 4 - b], lpsn.at[half, b], lprc.at[half, 4 - b], to))

    for half in range(2):
        for b in range(1, 4):
            arrived(p_in.at[half, b], prc.at[half, b])
            arrived(lp_in.at[half, b], lprc.at[half, b])
        levels = [lp_out[half, 0, 0:1, :]] + [lp_in[half, b, 0:1, :] for b in range(1, 4)]
        level, shares = combine(levels, None)
        values = [p_out[half, 0]] + [p_in[half, b] for b in range(1, 4)]
        z_out[half] = weighted(shares, values).astype(BF16)
        lz_out[half, 0:1, :] = level
        for i in (2 * half, 2 * half + 1):
            if i:
                to = dev(x, y, z + 4 * i, core)
                go(remote(z_out.at[half, pl.ds((i % 2) * 64, 64)], z_in.at[4 - i], zsn.at[i], zrc.at[4 - i], to))
                go(remote(lz_out.at[half], lz_in.at[4 - i], lzsn.at[i], lzrc.at[4 - i], to))

    for i in range(1, 4):
        arrived(z_in.at[i], zrc.at[i])
        arrived(lz_in.at[i], lzrc.at[i])
    levels = [expand(lz_out[0, 0:1, :])[:64]]
    levels += [expand(lz_in[i, 0:1, :])[(i % 2) * 64:(i % 2) * 64 + 64] for i in range(1, 4)]
    _, shares = combine(levels, None)
    result = shares[0] * z_out[0, 0:64, :].astype(F32)
    for i in range(1, 4):
        result = result + shares[i] * z_in[i].astype(F32)
    f_out[...] = result.reshape(8, 8, HEAD)
    for slot, (zt, c) in enumerate(sources, 1):
        go(remote(f_out.at[slot], f_in.at[my_group], fsn.at[slot], frc.at[my_group], dev(x, y, zt, c)))
    f_in[my_group] = f_out[0]
    for zt, c, _ in targets:
        group = group_of(zt, c)
        arrived(f_in.at[group], frc.at[group])
    for h in range(32):
        out_ref[:, h * HEAD:(h + 1) * HEAD] = f_in[h // 4, 2 * (h % 4):2 * (h % 4) + 2, :].astype(BF16)

    for copy in sends:
        copy.wait_send()
    for k in range(2, 8):
        for copy in result_copies(k):
            copy.wait_send()


def per_device(queries, keys, values, window_blocks):
    dma = pltpu.SemaphoreType.DMA
    vmem = pltpu.VMEM
    return pl.pallas_call(
        kernel,
        out_shape=jax.ShapeDtypeStruct(queries.shape, BF16),
        in_specs=[
            pl.BlockSpec(memory_space=pltpu.VMEM),
            pl.BlockSpec(memory_space=pl.ANY),
            pl.BlockSpec(memory_space=pl.ANY),
            pl.BlockSpec(memory_space=pltpu.SMEM),
        ],
        out_specs=pl.BlockSpec(memory_space=pltpu.VMEM),
        scratch_shapes=[
            vmem((8, 8, HEAD), F32), vmem((8, 8, HEAD), F32),
            vmem((8, 4, HEAD, HEAD), BF16), vmem((8, HEAD, HEAD), BF16), vmem((8, HEAD, 2 * HEAD), BF16),
            vmem((32, HEAD, HEAD), F32),
            vmem((8, 512, HEAD), BF16), vmem((8, 8, HEAD), F32), vmem((8, 512, HEAD), BF16), vmem((8, 8, HEAD), F32),
            vmem((2, 4, HEAD, HEAD), BF16), vmem((2, 4, 8, HEAD), F32),
            vmem((2, 4, HEAD, HEAD), BF16), vmem((2, 4, 8, HEAD), F32),
            vmem((2, HEAD, HEAD), BF16), vmem((2, 8, HEAD), F32),
            vmem((4, 64, HEAD), BF16), vmem((4, 8, HEAD), F32),
            vmem((8, 8, HEAD), F32), vmem((8, 8, HEAD), F32),
            dma((7,)), dma((8,)), dma((7,)), dma((8,)), dma((7,)), dma((8,)), dma((2,)),
            dma((4,)), dma((4,)), dma((2, 4)), dma((2, 4)), dma((8,)), dma((8,)),
            dma((8,)), dma((8,)), dma((8,)), dma((8,)),
            dma((2, 4)), dma((2, 4)), dma((2, 4)), dma((2, 4)),
            dma((4,)), dma((4,)), dma((4,)), dma((4,)), dma((8,)), dma((8,)),
        ],
        compiler_params=pltpu.CompilerParams(
            collective_id=0, has_side_effects=True, vmem_limit_bytes=40 * 1024 * 1024
        ),
    )(queries, keys, values, window_blocks)


def solution(mesh):
    return jax.shard_map(
        per_device,
        mesh=mesh,
        in_specs=(
            P(("row", "col", "uly"), None),
            P(("col", "row", "uly"), None),
            P(("col", "row", "uly"), None),
            P(),
        ),
        out_specs=P(("row", "col", "uly"), None),
        check_vma=False,
    )
```

```python
import math

import jax
import jax.numpy as jnp
from jax import lax
from jax.experimental import pallas as pl
from jax.experimental.pallas import tpu as pltpu
from jax.sharding import PartitionSpec as P

HEAD = 128
MESH = pl.DeviceIdType.MESH
SCALE = math.log2(math.e) / math.sqrt(HEAD)
HIDDEN = -1e30
F32, BF16 = jnp.float32, jnp.bfloat16
BLOCK = 128


def expand(row):
    return jnp.transpose(jnp.broadcast_to(row, (HEAD, HEAD)))


def combine(levels):
    top = jnp.maximum(jnp.maximum(levels[0], levels[1]), jnp.maximum(levels[2], levels[3]))
    shares = [jnp.exp2(level - top) for level in levels]
    total = (shares[0] + shares[1]) + (shares[2] + shares[3])
    inverse = 1.0 / total
    return top + jnp.log2(total), [share * inverse for share in shares]


def weighted(shares, values):
    acc = shares[0] * values[0].astype(F32)
    for share, value in zip(shares[1:], values[1:]):
        acc = acc + share * value.astype(F32)
    return acc


def kernel(
    q_ref, k_ref, v_ref, wb_ref, out_ref,
    wb, q_own, q_f32, q_cls, q_z, q_all, k_all, v_all, pos, thr, key_pos,
    o_all, l_all, o_in, l_in, p_out, lp_out, p_in, lp_in,
    z_out, lz_out, z_in, lz_in, s_out, s_in, f_in,
    own, swap, s1, s2, s3, q4s, q4r, kv, osn, orc, lsn, lrc, ps, lps, zs, lzs, fs,
):
    u = lax.axis_index("uly")
    row = lax.axis_index("row")
    col = lax.axis_index("col")
    x, core = row // 2, row % 2
    y = col % 4
    z = (col // 4) * 4 + u

    def dev(x_at, y_at, z_at, core_at):
        z_at = (z_at + 16) % 16
        return {
            "uly": z_at % 4,
            "row": (x_at % 4) * 2 + core_at,
            "col": (z_at // 4) * 4 + y_at % 4,
        }

    def remote(src, dst, sems, to):
        return pltpu.make_async_remote_copy(
            src_ref=src, dst_ref=dst, send_sem=sems[0], recv_sem=sems[1], device_id=to, device_id_type=MESH
        )

    other = dev(x, y, z, 1 - core)

    def pair(sem):
        return sem.at[0], sem.at[1]

    def arrived(ref, sems):
        remote(ref, ref, sems, other).wait_recv()

    def sent(ref, sems):
        remote(ref, ref, sems, other).wait_send()

    def loop(start, stop, body):
        def step(i, carry):
            body(i)
            return carry

        lax.fori_loop(start, stop, step, 0)

    d2 = 2 - 4 * core
    barrier = pltpu.get_barrier_semaphore()

    def greet(to):
        pl.semaphore_signal(barrier, inc=1, device_id=to, device_id_type=MESH)

    def greet_z(j):
        greet(dev(x, y, z + 5 - j, core))
        greet(dev(x, y, z - 5 + j, core))

    def greet_xy(i):
        greet(dev(x + i, y, z, core))
        greet(dev(x, y + i, z, core))

    loop(1, 5, greet_z)
    loop(1, 4, greet_xy)
    greet(dev(x, y, z + 1, 1 - core))
    greet(dev(x, y, z - 1, 1 - core))
    greet(dev(x, y, z + d2, 1 - core))
    greet(other)
    own_q = pltpu.make_async_copy(q_ref, q_own.at[0], own.at[0])
    own_q.start()
    own_wb = pltpu.make_async_copy(wb_ref, wb, own.at[1])
    own_wb.start()

    def features(ref, group):
        return ref.at[:, pl.ds(pl.multiple_of(group * HEAD, HEAD), HEAD)]

    def v_place(slot):
        return v_all.at[slot, :, pl.ds(0, HEAD)]

    my_group = 2 * u + core
    own_k = pltpu.make_async_copy(features(k_ref, my_group), k_all.at[0], own.at[2])
    own_v = pltpu.make_async_copy(features(v_ref, my_group), v_place(0), own.at[3])
    own_k.start()
    own_v.start()
    v_all[:, :, HEAD:] = jnp.ones((8, HEAD, HEAD), BF16)
    own_q.wait()
    own_wb.wait()
    pl.semaphore_wait(barrier, 18)

    remote(q_ref, q_own.at[1], pair(swap), other).start()
    arrived(q_own.at[1], pair(swap))

    def pack(c):
        for r in range(2):
            for g in range(4):
                at = pl.multiple_of(((2 * c + core) * 4 + g) * HEAD, HEAD)
                q_f32[c, 8 * r + 2 * g:8 * r + 2 * g + 2, :] = q_own[r, :, pl.ds(at, HEAD)].astype(F32)
        q_cls[c] = q_f32[c].astype(BF16)

    loop(0, 4, pack)

    def z_rows(at, n):
        return q_z.at[pl.ds(pl.multiple_of(16 * at, 16), 16 * n)]

    def along_z(j):
        d = 5 - j
        remote(q_cls.at[(u + d) % 4], z_rows(4 - d, 1), pair(s1), dev(x, y, z + d, core)).start()
        remote(q_cls.at[(u - d + 4) % 4], z_rows(4 + d, 1), pair(s1), dev(x, y, z - d, core)).start()

    loop(1, 5, along_z)
    q_z[64:80, :] = q_cls[u]

    def spread(group, slot, to):
        remote(features(k_ref, group), k_all.at[slot], (kv.at[0], kv.at[1]), to).start()
        remote(features(v_ref, group), v_place(slot), (kv.at[2], kv.at[3]), to).start()

    def spread_z(c):
        for d, slot in ((1, 2 + core), (-1, 4 + core), (d2, 6 + core)):
            spread(2 * ((u + d + 4) % 4) + c, slot, dev(x, y, z + d, c))

    loop(0, 2, spread_z)
    spread(2 * u + 1 - core, 1, other)

    blk = lax.broadcasted_iota(jnp.int32, (32, HEAD), 0)
    lane = lax.broadcasted_iota(jnp.int32, (32, HEAD), 1)
    half, step, sub = blk >> 4, (blk >> 2) & 3, blk & 3
    ys = (y + jnp.where(half == 0, step, sub)) & 3
    xs = (x + jnp.where(half == 0, sub, step)) & 3
    cs = jnp.where((lane & 8) == 0, core, 1 - core)
    z_src = (z + 8 * half + (lane >> 4) + 12) & 15
    which = 2 * (2 * xs + cs) + (z_src >> 3)
    block_at = jnp.zeros((32, HEAD), jnp.int32)
    for i in range(16):
        block_at = jnp.where(which == i, wb[i], block_at)
    within = (((z_src >> 2) & 1) * 4 + ys) * 8 + (z_src & 3) * 2 + (lane & 1)
    pos[...] = (64 * block_at + within).astype(F32)
    lane_f = lax.broadcasted_iota(jnp.int32, (1, HEAD), 1).astype(F32)
    sources = [(z, core), (z, 1 - core), (z - 1, 0), (z - 1, 1), (z + 1, 0), (z + 1, 1), (z - 2, 0), (z + 2, 1)]
    for j, (zt, c) in enumerate(sources):
        zt = (zt + 16) % 16
        base = (zt // 4) * 16384 + y * 4096 + x * 1024 + c * 512 + (zt % 4) * 128
        key_pos[j:j + 1, :] = lane_f + base.astype(F32)

    def spread_pos(b):
        thr[b] = expand(pos[pl.ds(b, 1), :])

    def first_peer(h, i):
        return dev(x + i * (1 - h), y + i * h, z, core)

    def second_peer(h, i):
        return dev(x + i * h, y + i * (1 - h), z, core)

    def first(h):
        def go(i):
            remote(q_z.at[pl.ds(128 * h, 128)], q_all.at[h, 0, 4 - i], (s3.at[h, 0], s3.at[h, 1]), first_peer(h, i)).start()

        loop(1, 4, go)
        q_all[h, 0, 0] = q_z[128 * h:128 * h + 128, :]

    def second(h):
        arrived(q_all.at[h, 0, pl.ds(1, 3)], (s3.at[h, 0], s3.at[h, 1]))

        def go(i):
            remote(q_all.at[h, 0], q_all.at[h, 4 - i], (q4s.at[h], q4r.at[h, 4 - i]), second_peer(h, i)).start()

        loop(1, 4, go)

    arrived(q_z.at[pl.ds(0, 128)], pair(s1))
    remote(z_rows(5, 4), z_rows(9, 4), pair(s2), dev(x, y, z - 4, core)).start()
    remote(z_rows(1, 3), z_rows(13, 3), pair(s2), dev(x, y, z + 4, core)).start()
    first(0)
    loop(0, 32, spread_pos)
    second(0)
    arrived(z_rows(9, 7), pair(s2))
    first(1)

    own_k.wait()
    own_v.wait()
    arrived(k_all.at[pl.ds(1, 7)], (kv.at[0], kv.at[1]))
    arrived(v_all.at[pl.ds(1, 7), :, pl.ds(0, HEAD)], (kv.at[2], kv.at[3]))

    eye = lax.broadcasted_iota(jnp.int32, (HEAD, HEAD), 0) == lax.broadcasted_iota(jnp.int32, (HEAD, HEAD), 1)

    def chunk(i):
        code = i - ((i + 6) // 8 - (i + 3) // 8) + 3 * ((i + 7) // 8 - (i + 6) // 8)
        h, t = code // 4, code % 4

        @pl.when(i == 1)
        def _():
            second(1)

        @pl.when(i >= 2)
        def _():
            arrived(q_all.at[h, t], (q4s.at[h], q4r.at[h, t]))

        def block(b):
            q = q_all[h, t, b]
            scores = lax.dot_general(
                q, k_all[...].reshape(1024, HEAD), (((1,), (1,)), ((), ())), preferred_element_type=F32
            )
            limit = thr[code * 4 + b]
            parts = [
                jnp.where(key_pos[j:j + 1, :] <= limit, scores[:, j * HEAD:(j + 1) * HEAD], HIDDEN) for j in range(8)
            ]
            top = parts[0]
            for part in parts[1:]:
                top = jnp.maximum(top, part)
            top = jnp.max(top, axis=1, keepdims=True) * SCALE
            weights = jnp.concatenate([jnp.exp2(part * SCALE - top).astype(BF16) for part in parts], axis=1)
            both = lax.dot_general(
                weights, v_all[...].reshape(1024, 2 * HEAD), (((1,), (0,)), ((), ())), preferred_element_type=F32
            )
            total = both[:, HEAD:]
            o_all[h, t, b] = (both[:, :HEAD] / total).astype(BF16)
            level = top + jnp.log2(total)
            l_all[h, t, pl.ds(b, 1), :] = jnp.sum(jnp.where(eye, level, 0.0), axis=0, keepdims=True)

        loop(0, 4, block)

        @pl.when(i >= 2)
        def _():
            to = second_peer(h, t)
            remote(o_all.at[h, t], o_in.at[h, 4 - t], (osn.at[h], orc.at[h]), to).start()
            remote(l_all.at[h, t], l_in.at[h, 4 - t], (lsn.at[h], lrc.at[h]), to).start()

    loop(0, 8, chunk)

    def join_second(h):
        arrived(o_in.at[h, pl.ds(1, 3)], (osn.at[h], orc.at[h]))
        arrived(l_in.at[h, pl.ds(1, 3)], (lsn.at[h], lrc.at[h]))

        def block(i):
            b = (i + 1) % 4
            level, shares = combine([l_all[h, 0, pl.ds(b, 1), :]] + [l_in[h, t, pl.ds(b, 1), :] for t in range(1, 4)])
            values = [o_all[h, 0, b]] + [o_in[h, t, b] for t in range(1, 4)]
            p_out[h, b] = weighted([expand(share) for share in shares], values).astype(BF16)
            lp_out[h, b] = level

            @pl.when(i < 3)
            def _():
                to = first_peer(h, b)
                remote(p_out.at[h, b], p_in.at[h, 4 - b], (ps.at[h, 0], ps.at[h, 1]), to).start()
                remote(lp_out.at[h, b], lp_in.at[h, 4 - b], (lps.at[h, 0], lps.at[h, 1]), to).start()

        loop(0, 4, block)

    loop(0, 2, join_second)

    def z_part(ref, s):
        return ref.at[pl.ds(pl.multiple_of(16 * s, 16), 16)]

    def join_first(h):
        arrived(p_in.at[h, pl.ds(1, 3)], (ps.at[h, 0], ps.at[h, 1]))
        arrived(lp_in.at[h, pl.ds(1, 3)], (lps.at[h, 0], lps.at[h, 1]))
        level, shares = combine([lp_out[h, 0]] + [lp_in[h, b] for b in range(1, 4)])
        values = [p_out[h, 0]] + [p_in[h, b] for b in range(1, 4)]
        joined = weighted([expand(share) for share in shares], values).astype(BF16)
        z_out[pl.ds(pl.multiple_of(128 * h, 128), 128), :] = joined
        lz_out[h] = level

        def go(i):
            s = 8 * h + i

            @pl.when(s != 4)
            def _():
                to = dev(x, y, z + s - 4, core)
                at = (20 - s) % 16
                remote(z_part(z_out, s), z_in.at[at], pair(zs), to).start()
                remote(lz_out.at[h], lz_in.at[at], pair(lzs), to).start()

        loop(0, 8, go)

    loop(0, 2, join_first)
    z_in[0] = z_out[64:80, :]
    lz_in[0] = lz_out[0]
    arrived(z_in.at[pl.ds(1, 15)], pair(zs))
    arrived(lz_in.at[pl.ds(1, 15)], pair(lzs))
    lane16 = lax.broadcasted_iota(jnp.int32, (16, HEAD), 1) - lax.broadcasted_iota(jnp.int32, (16, HEAD), 0)

    def join_z(w):
        levels, values = [], []
        for m in range(4):
            at = w + 4 * m
            offset = ((20 - at) % 8) * 16
            wide = jnp.broadcast_to(lz_in[at], (16, HEAD))
            levels.append(jnp.sum(jnp.where(lane16 == offset, wide, 0.0), axis=1, keepdims=True))
            values.append(z_in[at])
        _, shares = combine(levels)
        joined = weighted(shares, values)
        f_in[2 * ((u + w) % 4) + core] = joined[:8]
        s_out[w] = joined[8:]

    loop(0, 4, join_z)
    remote(s_out, s_in, pair(fs), other).start()
    arrived(s_in, pair(fs))

    def place(w):
        f_in[2 * ((u + w) % 4) + 1 - core] = s_in[w]

    loop(0, 4, place)

    def give(c):
        for g in range(4):
            at = pl.multiple_of((4 * c + g) * HEAD, HEAD)
            out_ref[:, pl.ds(at, HEAD)] = f_in[c, 2 * g:2 * g + 2, :].astype(BF16)

    loop(0, 8, give)

    sent(q_own.at[1], pair(swap))
    sent(q_z.at[pl.ds(0, 128)], pair(s1))
    sent(z_rows(9, 7), pair(s2))
    sent(k_all.at[pl.ds(1, 7)], (kv.at[0], kv.at[1]))
    sent(v_all.at[pl.ds(1, 7), :, pl.ds(0, HEAD)], (kv.at[2], kv.at[3]))
    for h in range(2):
        sent(q_all.at[h, 0, pl.ds(1, 3)], (s3.at[h, 0], s3.at[h, 1]))
        sent(q_all.at[h, pl.ds(1, 3)], (q4s.at[h], q4r.at[h, 0]))
        sent(o_in.at[h, pl.ds(1, 3)], (osn.at[h], orc.at[h]))
        sent(l_in.at[h, pl.ds(1, 3)], (lsn.at[h], lrc.at[h]))
        sent(p_in.at[h, pl.ds(1, 3)], (ps.at[h, 0], ps.at[h, 1]))
        sent(lp_in.at[h, pl.ds(1, 3)], (lps.at[h, 0], lps.at[h, 1]))
    sent(z_in.at[pl.ds(1, 15)], pair(zs))
    sent(lz_in.at[pl.ds(1, 15)], pair(lzs))
    sent(s_in, pair(fs))


def per_device(queries, keys, values, window_blocks):
    dma = pltpu.SemaphoreType.DMA
    vmem = pltpu.VMEM
    return pl.pallas_call(
        kernel,
        out_shape=jax.ShapeDtypeStruct(queries.shape, BF16),
        in_specs=[pl.BlockSpec(memory_space=pl.ANY)] * 4,
        out_specs=pl.BlockSpec(memory_space=pltpu.VMEM),
        scratch_shapes=[
            pltpu.SMEM((16,), jnp.int32),
            vmem((2, 2, 4096), BF16), vmem((4, 16, HEAD), F32), vmem((4, 16, HEAD), BF16), vmem((256, HEAD), BF16),
            vmem((2, 4, 4, HEAD, HEAD), BF16), vmem((8, HEAD, HEAD), BF16), vmem((8, HEAD, 2 * HEAD), BF16),
            vmem((32, HEAD), F32), vmem((32, HEAD, HEAD), F32), vmem((8, HEAD), F32),
            vmem((2, 4, 4, HEAD, HEAD), BF16), vmem((2, 4, 4, HEAD), F32),
            vmem((2, 4, 4, HEAD, HEAD), BF16), vmem((2, 4, 4, HEAD), F32),
            vmem((2, 4, HEAD, HEAD), BF16), vmem((2, 4, 1, HEAD), F32),
            vmem((2, 4, HEAD, HEAD), BF16), vmem((2, 4, 1, HEAD), F32),
            vmem((256, HEAD), BF16), vmem((2, 1, HEAD), F32),
            vmem((16, 16, HEAD), BF16), vmem((16, 1, HEAD), F32),
            vmem((4, 8, HEAD), F32), vmem((4, 8, HEAD), F32), vmem((8, 8, HEAD), F32),
            dma((4,)), dma((2,)), dma((2,)), dma((2,)), dma((2, 2)), dma((2,)), dma((2, 4)), dma((4,)),
            dma((2,)), dma((2,)), dma((2,)), dma((2,)), dma((2, 2)), dma((2, 2)), dma((2,)), dma((2,)), dma((2,)),
        ],
        compiler_params=pltpu.CompilerParams(
            collective_id=0, has_side_effects=True, vmem_limit_bytes=58 * 1024 * 1024
        ),
    )(queries, keys, values, window_blocks)


def solution(mesh):
    return jax.shard_map(
        per_device,
        mesh=mesh,
        in_specs=(
            P(("row", "col", "uly"), None),
            P(("col", "row", "uly"), None),
            P(("col", "row", "uly"), None),
            P(),
        ),
        out_specs=P(("row", "col", "uly"), None),
        check_vma=False,
    )
```

```python
import math

import jax
import jax.numpy as jnp
from jax import lax
from jax.experimental import pallas as pl
from jax.experimental.pallas import tpu as pltpu
from jax.sharding import PartitionSpec as P

HEAD = 128
MESH = pl.DeviceIdType.MESH
SCALE = math.log2(math.e) / math.sqrt(HEAD)
HIDDEN = -1e30
F32, BF16 = jnp.float32, jnp.bfloat16


def expand(row):
    return jnp.transpose(jnp.broadcast_to(row, (HEAD, HEAD)))


def combine(levels):
    top = jnp.maximum(jnp.maximum(levels[0], levels[1]), jnp.maximum(levels[2], levels[3]))
    shares = [jnp.exp2(level - top) for level in levels]
    total = (shares[0] + shares[1]) + (shares[2] + shares[3])
    inverse = 1.0 / total
    return top + jnp.log2(total), [share * inverse for share in shares]


def weighted(shares, values):
    acc = shares[0] * values[0].astype(F32)
    for share, value in zip(shares[1:], values[1:]):
        acc = acc + share * value.astype(F32)
    return acc


def kernel(
    q_ref, k_ref, v_ref, wb_ref, out_ref,
    wb, q_own, q_f32, q_cls, q_z, q_all, k_all, v_all, pos, thr, key_pos,
    o_all, l_all, o_in, l_in, p_out, lp_out, p_in, lp_in,
    z_out, lz_out, z_in, lz_in, s_out, s_in, f_in,
    own, swap, s1, s2, s3, q4s, q4r, kv, osn, orc, lsn, lrc, ps, lps, zs, lzs, fs,
):
    u = lax.axis_index("uly")
    row = lax.axis_index("row")
    col = lax.axis_index("col")
    x, core = row // 2, row % 2
    y = col % 4
    z = (col // 4) * 4 + u

    def dev(x_at, y_at, z_at, core_at):
        z_at = (z_at + 16) % 16
        return {
            "uly": z_at % 4,
            "row": (x_at % 4) * 2 + core_at,
            "col": (z_at // 4) * 4 + y_at % 4,
        }

    def remote(src, dst, sems, to):
        return pltpu.make_async_remote_copy(
            src_ref=src, dst_ref=dst, send_sem=sems[0], recv_sem=sems[1], device_id=to, device_id_type=MESH
        )

    other = dev(x, y, z, 1 - core)

    def pair(sem):
        return sem.at[0], sem.at[1]

    def arrived(ref, sems):
        remote(ref, ref, sems, other).wait_recv()

    def sent(ref, sems):
        remote(ref, ref, sems, other).wait_send()

    def loop(start, stop, body):
        def step(i, carry):
            body(i)
            return carry

        lax.fori_loop(start, stop, step, 0)

    d2 = 2 - 4 * core
    barrier = pltpu.get_barrier_semaphore()

    def greet(to):
        pl.semaphore_signal(barrier, inc=1, device_id=to, device_id_type=MESH)

    def greet_z(j):
        greet(dev(x, y, z + 5 - j, core))
        greet(dev(x, y, z - 5 + j, core))

    def greet_xy(i):
        greet(dev(x + i, y, z, core))
        greet(dev(x, y + i, z, core))

    loop(1, 5, greet_z)
    loop(1, 4, greet_xy)
    greet(dev(x, y, z + 1, 1 - core))
    greet(dev(x, y, z - 1, 1 - core))
    greet(dev(x, y, z + d2, 1 - core))
    greet(other)
    own_q = pltpu.make_async_copy(q_ref, q_own.at[0], own.at[0])
    own_q.start()
    own_wb = pltpu.make_async_copy(wb_ref, wb, own.at[1])
    own_wb.start()

    def features(ref, group):
        return ref.at[:, pl.ds(pl.multiple_of(group * HEAD, HEAD), HEAD)]

    def v_place(slot):
        return v_all.at[slot, :, pl.ds(0, HEAD)]

    my_group = 2 * u + core
    own_k = pltpu.make_async_copy(features(k_ref, my_group), k_all.at[0], own.at[2])
    own_v = pltpu.make_async_copy(features(v_ref, my_group), v_place(0), own.at[3])
    own_k.start()
    own_v.start()
    v_all[:, :, HEAD:] = jnp.ones((8, HEAD, HEAD), BF16)
    own_q.wait()
    own_wb.wait()
    pl.semaphore_wait(barrier, 18)

    remote(q_ref, q_own.at[1], pair(swap), other).start()
    arrived(q_own.at[1], pair(swap))

    def pack(c):
        for r in range(2):
            for g in range(4):
                at = pl.multiple_of(((2 * c + core) * 4 + g) * HEAD, HEAD)
                q_f32[c, 8 * r + 2 * g:8 * r + 2 * g + 2, :] = q_own[r, :, pl.ds(at, HEAD)].astype(F32)
        q_cls[c] = q_f32[c].astype(BF16)

    loop(0, 4, pack)

    def z_rows(at, n):
        return q_z.at[pl.ds(pl.multiple_of(16 * at, 16), 16 * n)]

    def along_z(j):
        d = 5 - j
        remote(q_cls.at[(u + d) % 4], z_rows(4 - d, 1), pair(s1), dev(x, y, z + d, core)).start()
        remote(q_cls.at[(u - d + 4) % 4], z_rows(4 + d, 1), pair(s1), dev(x, y, z - d, core)).start()

    loop(1, 5, along_z)
    q_z[64:80, :] = q_cls[u]

    blk = lax.broadcasted_iota(jnp.int32, (32, HEAD), 0)
    lane = lax.broadcasted_iota(jnp.int32, (32, HEAD), 1)
    half, step, sub = blk >> 4, (blk >> 2) & 3, blk & 3
    ys = (y + jnp.where(half == 0, step, sub)) & 3
    xs = (x + jnp.where(half == 0, sub, step)) & 3
    cs = jnp.where((lane & 8) == 0, core, 1 - core)
    z_src = (z + 8 * half + (lane >> 4) + 12) & 15
    which = 2 * (2 * xs + cs) + (z_src >> 3)
    block_at = jnp.zeros((32, HEAD), jnp.int32)
    for i in range(16):
        block_at = jnp.where(which == i, wb[i], block_at)
    within = (((z_src >> 2) & 1) * 4 + ys) * 8 + (z_src & 3) * 2 + (lane & 1)
    pos[...] = (64 * block_at + within).astype(F32)
    lane_f = lax.broadcasted_iota(jnp.int32, (1, HEAD), 1).astype(F32)
    sources = [(z, core), (z, 1 - core), (z - 1, 0), (z - 1, 1), (z + 1, 0), (z + 1, 1), (z - 2, 0), (z + 2, 1)]
    for j, (zt, c) in enumerate(sources):
        zt = (zt + 16) % 16
        base = (zt // 4) * 16384 + y * 4096 + x * 1024 + c * 512 + (zt % 4) * 128
        key_pos[j:j + 1, :] = lane_f + base.astype(F32)

    def spread_pos(b):
        thr[b] = expand(pos[pl.ds(b, 1), :])

    def first_peer(h, i):
        return dev(x + i * (1 - h), y + i * h, z, core)

    def second_peer(h, i):
        return dev(x + i * h, y + i * (1 - h), z, core)

    def first(h):
        mine = q_z.at[pl.ds(128 * h, 128)]

        def go(i):
            remote(mine, q_all.at[h, 0, 4 - i], (s3.at[h, 0], s3.at[h, 4 - i]), first_peer(h, i)).start()

        def go_on(i):
            remote(mine, q_all.at[h, 4 - i, 0], (q4s.at[h], q4r.at[h, 4 - i]), second_peer(h, i)).start()

        loop(1, 4, go)
        loop(1, 4, go_on)
        q_all[h, 0, 0] = q_z[128 * h:128 * h + 128, :]

    def second(h):
        def pass_on(j):
            r = j + j // 2 - 2 * (j // 3)
            arrived(q_all.at[h, 0, r], (s3.at[h, 0], s3.at[h, r]))

            def go(i):
                remote(q_all.at[h, 0, r], q_all.at[h, 4 - i, r], (q4s.at[h], q4r.at[h, 4 - i]), second_peer(h, i)).start()

            loop(1, 4, go)

        loop(1, 4, pass_on)

    arrived(q_z.at[pl.ds(0, 128)], pair(s1))
    remote(z_rows(5, 4), z_rows(9, 4), pair(s2), dev(x, y, z - 4, core)).start()
    remote(z_rows(1, 3), z_rows(13, 3), pair(s2), dev(x, y, z + 4, core)).start()
    first(0)

    def spread(group, slot, to):
        remote(features(k_ref, group), k_all.at[slot], (kv.at[0], kv.at[1]), to).start()
        remote(features(v_ref, group), v_place(slot), (kv.at[2], kv.at[3]), to).start()

    def spread_z(c):
        for d, slot in ((1, 2 + core), (-1, 4 + core), (d2, 6 + core)):
            spread(2 * ((u + d + 4) % 4) + c, slot, dev(x, y, z + d, c))

    loop(0, 2, spread_z)
    spread(2 * u + 1 - core, 1, other)

    loop(0, 32, spread_pos)
    second(0)
    arrived(z_rows(9, 7), pair(s2))
    first(1)
    second(1)

    own_k.wait()
    own_v.wait()
    arrived(k_all.at[pl.ds(1, 7)], (kv.at[0], kv.at[1]))
    arrived(v_all.at[pl.ds(1, 7), :, pl.ds(0, HEAD)], (kv.at[2], kv.at[3]))

    eye = lax.broadcasted_iota(jnp.int32, (HEAD, HEAD), 0) == lax.broadcasted_iota(jnp.int32, (HEAD, HEAD), 1)

    def chunk(i):
        h, t = i // 4, i % 4

        @pl.when(t > 0)
        def _():
            arrived(q_all.at[h, t], (q4s.at[h], q4r.at[h, t]))

        for b in (0, 2):
            q = q_all[h, t, b:b + 2].reshape(256, HEAD)
            scores = lax.dot_general(
                q, k_all[...].reshape(1024, HEAD), (((1,), (1,)), ((), ())), preferred_element_type=F32
            )
            limit = thr[pl.ds(4 * i + b, 2)].reshape(256, HEAD)
            parts = [
                jnp.where(key_pos[j:j + 1, :] <= limit, scores[:, j * HEAD:(j + 1) * HEAD], HIDDEN) for j in range(8)
            ]
            top = parts[0]
            for part in parts[1:]:
                top = jnp.maximum(top, part)
            top = jnp.max(top, axis=1, keepdims=True) * SCALE
            weights = jnp.concatenate([jnp.exp2(part * SCALE - top).astype(BF16) for part in parts], axis=1)
            both = lax.dot_general(
                weights, v_all[...].reshape(1024, 2 * HEAD), (((1,), (0,)), ((), ())), preferred_element_type=F32
            )
            total = both[:, HEAD:]
            o_all[h, t, b:b + 2] = (both[:, :HEAD] / total).astype(BF16).reshape(2, HEAD, HEAD)
            level = top + jnp.log2(total)
            for r in range(2):
                l_all[h, t, b + r:b + r + 1, :] = jnp.sum(
                    jnp.where(eye, level[r * HEAD:(r + 1) * HEAD], 0.0), axis=0, keepdims=True
                )

        @pl.when(t > 0)
        def _():
            to = second_peer(h, t)
            remote(o_all.at[h, t], o_in.at[h, 4 - t], (osn.at[h], orc.at[h]), to).start()
            remote(l_all.at[h, t], l_in.at[h, 4 - t], (lsn.at[h], lrc.at[h]), to).start()

    loop(0, 8, chunk)

    def join_second(h):
        arrived(o_in.at[h, pl.ds(1, 3)], (osn.at[h], orc.at[h]))
        arrived(l_in.at[h, pl.ds(1, 3)], (lsn.at[h], lrc.at[h]))

        def block(i):
            b = (i + 1) % 4
            level, shares = combine([l_all[h, 0, pl.ds(b, 1), :]] + [l_in[h, t, pl.ds(b, 1), :] for t in range(1, 4)])
            values = [o_all[h, 0, b]] + [o_in[h, t, b] for t in range(1, 4)]
            p_out[h, b] = weighted([expand(share) for share in shares], values).astype(BF16)
            lp_out[h, b] = level

            @pl.when(i < 3)
            def _():
                to = first_peer(h, b)
                remote(p_out.at[h, b], p_in.at[h, 4 - b], (ps.at[h, 0], ps.at[h, 1]), to).start()
                remote(lp_out.at[h, b], lp_in.at[h, 4 - b], (lps.at[h, 0], lps.at[h, 1]), to).start()

        loop(0, 4, block)

    loop(0, 2, join_second)

    def z_part(ref, s):
        return ref.at[pl.ds(pl.multiple_of(16 * s, 16), 16)]

    def join_first(h):
        arrived(p_in.at[h, pl.ds(1, 3)], (ps.at[h, 0], ps.at[h, 1]))
        arrived(lp_in.at[h, pl.ds(1, 3)], (lps.at[h, 0], lps.at[h, 1]))
        level, shares = combine([lp_out[h, 0]] + [lp_in[h, b] for b in range(1, 4)])
        values = [p_out[h, 0]] + [p_in[h, b] for b in range(1, 4)]
        joined = weighted([expand(share) for share in shares], values).astype(BF16)
        z_out[pl.ds(pl.multiple_of(128 * h, 128), 128), :] = joined
        lz_out[h] = level

        def go(i):
            s = 8 * h + (i + 4 * h) % 8

            @pl.when(s != 4)
            def _():
                to = dev(x, y, z + s - 4, core)
                at = (20 - s) % 16
                remote(z_part(z_out, s), z_in.at[at], pair(zs), to).start()
                remote(lz_out.at[h], lz_in.at[at], pair(lzs), to).start()

        loop(0, 8, go)

    loop(0, 2, join_first)
    z_in[0] = z_out[64:80, :]
    lz_in[0] = lz_out[0]
    arrived(z_in.at[pl.ds(1, 15)], pair(zs))
    arrived(lz_in.at[pl.ds(1, 15)], pair(lzs))
    lane16 = lax.broadcasted_iota(jnp.int32, (16, HEAD), 1) - lax.broadcasted_iota(jnp.int32, (16, HEAD), 0)

    def join_z(w):
        levels, values = [], []
        for m in range(4):
            at = w + 4 * m
            offset = ((20 - at) % 8) * 16
            wide = jnp.broadcast_to(lz_in[at], (16, HEAD))
            levels.append(jnp.sum(jnp.where(lane16 == offset, wide, 0.0), axis=1, keepdims=True))
            values.append(z_in[at])
        _, shares = combine(levels)
        joined = weighted(shares, values)
        f_in[2 * ((u + w) % 4) + core] = joined[:8]
        s_out[w] = joined[8:]

    loop(0, 4, join_z)
    remote(s_out, s_in, pair(fs), other).start()
    arrived(s_in, pair(fs))

    def place(w):
        f_in[2 * ((u + w) % 4) + 1 - core] = s_in[w]

    loop(0, 4, place)

    def give(c):
        for g in range(4):
            at = pl.multiple_of((4 * c + g) * HEAD, HEAD)
            out_ref[:, pl.ds(at, HEAD)] = f_in[c, 2 * g:2 * g + 2, :].astype(BF16)

    loop(0, 8, give)

    sent(q_own.at[1], pair(swap))
    sent(q_z.at[pl.ds(0, 128)], pair(s1))
    sent(z_rows(9, 7), pair(s2))
    sent(k_all.at[pl.ds(1, 7)], (kv.at[0], kv.at[1]))
    sent(v_all.at[pl.ds(1, 7), :, pl.ds(0, HEAD)], (kv.at[2], kv.at[3]))
    for h in range(2):
        sent(q_all.at[h, 0, pl.ds(1, 3)], (s3.at[h, 0], s3.at[h, 1]))
        sent(q_all.at[h, pl.ds(1, 3)], (q4s.at[h], q4r.at[h, 0]))
        sent(o_in.at[h, pl.ds(1, 3)], (osn.at[h], orc.at[h]))
        sent(l_in.at[h, pl.ds(1, 3)], (lsn.at[h], lrc.at[h]))
        sent(p_in.at[h, pl.ds(1, 3)], (ps.at[h, 0], ps.at[h, 1]))
        sent(lp_in.at[h, pl.ds(1, 3)], (lps.at[h, 0], lps.at[h, 1]))
    sent(z_in.at[pl.ds(1, 15)], pair(zs))
    sent(lz_in.at[pl.ds(1, 15)], pair(lzs))
    sent(s_in, pair(fs))


def per_device(queries, keys, values, window_blocks):
    dma = pltpu.SemaphoreType.DMA
    vmem = pltpu.VMEM
    return pl.pallas_call(
        kernel,
        out_shape=jax.ShapeDtypeStruct(queries.shape, BF16),
        in_specs=[pl.BlockSpec(memory_space=pl.ANY)] * 4,
        out_specs=pl.BlockSpec(memory_space=pltpu.VMEM),
        scratch_shapes=[
            pltpu.SMEM((16,), jnp.int32),
            vmem((2, 2, 4096), BF16), vmem((4, 16, HEAD), F32), vmem((4, 16, HEAD), BF16), vmem((256, HEAD), BF16),
            vmem((2, 4, 4, HEAD, HEAD), BF16), vmem((8, HEAD, HEAD), BF16), vmem((8, HEAD, 2 * HEAD), BF16),
            vmem((32, HEAD), F32), vmem((32, HEAD, HEAD), F32), vmem((8, HEAD), F32),
            vmem((2, 4, 4, HEAD, HEAD), BF16), vmem((2, 4, 4, HEAD), F32),
            vmem((2, 4, 4, HEAD, HEAD), BF16), vmem((2, 4, 4, HEAD), F32),
            vmem((2, 4, HEAD, HEAD), BF16), vmem((2, 4, 1, HEAD), F32),
            vmem((2, 4, HEAD, HEAD), BF16), vmem((2, 4, 1, HEAD), F32),
            vmem((256, HEAD), BF16), vmem((2, 1, HEAD), F32),
            vmem((16, 16, HEAD), BF16), vmem((16, 1, HEAD), F32),
            vmem((4, 8, HEAD), F32), vmem((4, 8, HEAD), F32), vmem((8, 8, HEAD), F32),
            dma((4,)), dma((2,)), dma((2,)), dma((2,)), dma((2, 4)), dma((2,)), dma((2, 4)), dma((4,)),
            dma((2,)), dma((2,)), dma((2,)), dma((2,)), dma((2, 2)), dma((2, 2)), dma((2,)), dma((2,)), dma((2,)),
        ],
        compiler_params=pltpu.CompilerParams(
            collective_id=0, has_side_effects=True, vmem_limit_bytes=58 * 1024 * 1024
        ),
    )(queries, keys, values, window_blocks)


def solution(mesh):
    return jax.shard_map(
        per_device,
        mesh=mesh,
        in_specs=(
            P(("row", "col", "uly"), None),
            P(("col", "row", "uly"), None),
            P(("col", "row", "uly"), None),
            P(),
        ),
        out_specs=P(("row", "col", "uly"), None),
        check_vma=False,
    )
```

```python
import math

import jax
import jax.numpy as jnp
from jax import lax
from jax.experimental import pallas as pl
from jax.experimental.pallas import tpu as pltpu
from jax.sharding import PartitionSpec as P

HEAD = 128
MESH = pl.DeviceIdType.MESH
SCALE = math.log2(math.e) / math.sqrt(HEAD)
HIDDEN = -1e30
F32, BF16 = jnp.float32, jnp.bfloat16


def expand(row):
    return jnp.transpose(jnp.broadcast_to(row, (HEAD, HEAD)))


def combine(levels):
    top = jnp.maximum(jnp.maximum(levels[0], levels[1]), jnp.maximum(levels[2], levels[3]))
    shares = [jnp.exp2(level - top) for level in levels]
    total = (shares[0] + shares[1]) + (shares[2] + shares[3])
    inverse = 1.0 / total
    return top + jnp.log2(total), [share * inverse for share in shares]


def weighted(shares, values):
    acc = shares[0] * values[0].astype(F32)
    for share, value in zip(shares[1:], values[1:]):
        acc = acc + share * value.astype(F32)
    return acc


def kernel(
    q_ref, k_ref, v_ref, wb_ref, out_ref,
    wb, q_own, q_f32, q_cls, q_z, q_all, k_all, v_all, pos, thr, key_pos,
    o_all, l_all, o_in, l_in, p_out, lp_out, p_in, lp_in,
    z_out, lz_out, z_in, lz_in, s_out, s_in, f_in,
    own, swap, s1, s2, s3, s3r, q4s, q4r, kv, osn, orc, lsn, lrc, ps, lps, zs, lzs, fs,
):
    u = lax.axis_index("uly")
    row = lax.axis_index("row")
    col = lax.axis_index("col")
    x, core = row // 2, row % 2
    y = col % 4
    z = (col // 4) * 4 + u

    def dev(x_at, y_at, z_at, core_at):
        z_at = (z_at + 16) % 16
        return {
            "uly": z_at % 4,
            "row": (x_at % 4) * 2 + core_at,
            "col": (z_at // 4) * 4 + y_at % 4,
        }

    def remote(src, dst, sems, to):
        return pltpu.make_async_remote_copy(
            src_ref=src, dst_ref=dst, send_sem=sems[0], recv_sem=sems[1], device_id=to, device_id_type=MESH
        )

    other = dev(x, y, z, 1 - core)

    def pair(sem):
        return sem.at[0], sem.at[1]

    def arrived(ref, sems):
        remote(ref, ref, sems, other).wait_recv()

    def sent(ref, sems):
        remote(ref, ref, sems, other).wait_send()

    def loop(start, stop, body):
        def step(i, carry):
            body(i)
            return carry

        lax.fori_loop(start, stop, step, 0)

    d2 = 2 - 4 * core
    barrier = pltpu.get_barrier_semaphore()

    def greet(to):
        pl.semaphore_signal(barrier, inc=1, device_id=to, device_id_type=MESH)

    def greet_z(j):
        greet(dev(x, y, z + 5 - j, core))
        greet(dev(x, y, z - 5 + j, core))

    def greet_xy(i):
        greet(dev(x + i, y, z, core))
        greet(dev(x, y + i, z, core))

    loop(1, 5, greet_z)
    loop(1, 4, greet_xy)
    greet(dev(x, y, z + 1, 1 - core))
    greet(dev(x, y, z - 1, 1 - core))
    greet(dev(x, y, z + d2, 1 - core))
    greet(other)
    own_q = pltpu.make_async_copy(q_ref, q_own.at[0], own.at[0])
    own_q.start()
    own_wb = pltpu.make_async_copy(wb_ref, wb, own.at[1])
    own_wb.start()

    def features(ref, group):
        return ref.at[:, pl.ds(pl.multiple_of(group * HEAD, HEAD), HEAD)]

    def v_place(slot):
        return v_all.at[slot, :, pl.ds(0, HEAD)]

    my_group = 2 * u + core
    own_k = pltpu.make_async_copy(features(k_ref, my_group), k_all.at[0], own.at[2])
    own_v = pltpu.make_async_copy(features(v_ref, my_group), v_place(0), own.at[3])
    own_k.start()
    own_v.start()
    v_all[:, :, HEAD:] = jnp.ones((8, HEAD, HEAD), BF16)
    pl.semaphore_wait(barrier, 18)

    remote(q_ref, q_own.at[1], pair(swap), other).start()
    own_q.wait()
    own_wb.wait()
    arrived(q_own.at[1], pair(swap))

    def pack(c):
        for r in range(2):
            for g in range(4):
                at = pl.multiple_of(((2 * c + core) * 4 + g) * HEAD, HEAD)
                q_f32[c, 8 * r + 2 * g:8 * r + 2 * g + 2, :] = q_own[r, :, pl.ds(at, HEAD)].astype(F32)
        q_cls[c] = q_f32[c].astype(BF16)

    loop(0, 4, pack)

    def z_rows(at, n):
        return q_z.at[pl.ds(pl.multiple_of(16 * at, 16), 16 * n)]

    def along_z(j):
        d = 5 - j
        remote(q_cls.at[(u + d) % 4], z_rows(4 - d, 1), pair(s1), dev(x, y, z + d, core)).start()
        remote(q_cls.at[(u - d + 4) % 4], z_rows(4 + d, 1), pair(s1), dev(x, y, z - d, core)).start()

    loop(1, 5, along_z)
    q_z[64:80, :] = q_cls[u]

    blk = lax.broadcasted_iota(jnp.int32, (32, HEAD), 0)
    lane = lax.broadcasted_iota(jnp.int32, (32, HEAD), 1)
    half, step, side, sub = blk >> 4, (blk >> 2) & 3, (blk >> 1) & 1, 2 * (blk & 1) + (lane >> 6)
    ys = (y + jnp.where(side == 0, step, sub)) & 3
    xs = (x + jnp.where(side == 0, sub, step)) & 3
    cs = jnp.where((lane & 8) == 0, core, 1 - core)
    z_src = (z + 8 * half + 4 * side + ((lane >> 4) & 3) + 12) & 15
    which = 2 * (2 * xs + cs) + (z_src >> 3)
    block_at = jnp.zeros((32, HEAD), jnp.int32)
    for i in range(16):
        block_at = jnp.where(which == i, wb[i], block_at)
    within = (((z_src >> 2) & 1) * 4 + ys) * 8 + (z_src & 3) * 2 + (lane & 1)
    pos[...] = (64 * block_at + within).astype(F32)
    lane_f = lax.broadcasted_iota(jnp.int32, (1, HEAD), 1).astype(F32)
    sources = [(z, core), (z, 1 - core), (z - 1, 0), (z - 1, 1), (z + 1, 0), (z + 1, 1), (z - 2, 0), (z + 2, 1)]
    for j, (zt, c) in enumerate(sources):
        zt = (zt + 16) % 16
        base = (zt // 4) * 16384 + y * 4096 + x * 1024 + c * 512 + (zt % 4) * 128
        key_pos[j:j + 1, :] = lane_f + base.astype(F32)

    def spread_pos(b):
        thr[b] = expand(pos[pl.ds(b, 1), :])

    def first_peer(a, i):
        return dev(x + i * (1 - a), y + i * a, z, core)

    def second_peer(a, i):
        return dev(x + i * a, y + i * (1 - a), z, core)

    def first(h):
        for a in range(2):
            mine = q_z.at[pl.ds(128 * h + 64 * a, 64)]

            def go(i):
                remote(mine, q_all.at[h, 0, a, 4 - i], (s3.at[h], s3r.at[h, a, 4 - i]), first_peer(a, i)).start()

            loop(1, 4, go)
        for a in range(2):
            mine = q_z.at[pl.ds(128 * h + 64 * a, 64)]

            def go_on(i):
                remote(mine, q_all.at[h, 4 - i, a, 0], (q4s.at[h], q4r.at[h, 4 - i]), second_peer(a, i)).start()

            loop(1, 4, go_on)
            q_all[h, 0, a, 0] = q_z[128 * h + 64 * a:128 * h + 64 * a + 64, :]

    def second(h):
        def pass_on(j):
            r = j + j // 2 - 2 * (j // 3)
            for a in range(2):
                block = q_all.at[h, 0, a, r]
                arrived(block, (s3.at[h], s3r.at[h, a, r]))

                def go(i):
                    remote(block, q_all.at[h, 4 - i, a, r], (q4s.at[h], q4r.at[h, 4 - i]), second_peer(a, i)).start()

                loop(1, 4, go)

        loop(1, 4, pass_on)

    arrived(q_z.at[pl.ds(0, 128)], pair(s1))
    remote(z_rows(5, 4), z_rows(9, 4), pair(s2), dev(x, y, z - 4, core)).start()
    remote(z_rows(1, 3), z_rows(13, 3), pair(s2), dev(x, y, z + 4, core)).start()
    first(0)

    def spread(group, slot, to):
        remote(features(k_ref, group), k_all.at[slot], (kv.at[0], kv.at[1]), to).start()
        remote(features(v_ref, group), v_place(slot), (kv.at[2], kv.at[3]), to).start()

    def spread_z(c):
        for d, slot in ((1, 2 + core), (-1, 4 + core), (d2, 6 + core)):
            spread(2 * ((u + d + 4) % 4) + c, slot, dev(x, y, z + d, c))

    loop(0, 2, spread_z)
    spread(2 * u + 1 - core, 1, other)

    loop(0, 32, spread_pos)
    second(0)
    arrived(z_rows(9, 7), pair(s2))
    first(1)
    second(1)

    own_k.wait()
    own_v.wait()
    arrived(k_all.at[pl.ds(1, 7)], (kv.at[0], kv.at[1]))
    arrived(v_all.at[pl.ds(1, 7), :, pl.ds(0, HEAD)], (kv.at[2], kv.at[3]))

    eye = lax.broadcasted_iota(jnp.int32, (HEAD, HEAD), 0) == lax.broadcasted_iota(jnp.int32, (HEAD, HEAD), 1)

    def chunk(i):
        h, t = i // 4, i % 4

        @pl.when(t > 0)
        def _():
            arrived(q_all.at[h, t], (q4s.at[h], q4r.at[h, t]))

        for a in range(2):
            q = q_all[h, t, a].reshape(256, HEAD)
            scores = lax.dot_general(
                q, k_all[...].reshape(1024, HEAD), (((1,), (1,)), ((), ())), preferred_element_type=F32
            )
            limit = thr[pl.ds(4 * i + 2 * a, 2)].reshape(256, HEAD)
            parts = [
                jnp.where(key_pos[j:j + 1, :] <= limit, scores[:, j * HEAD:(j + 1) * HEAD], HIDDEN) for j in range(8)
            ]
            top = parts[0]
            for part in parts[1:]:
                top = jnp.maximum(top, part)
            top = jnp.max(top, axis=1, keepdims=True) * SCALE
            weights = jnp.concatenate([jnp.exp2(part * SCALE - top).astype(BF16) for part in parts], axis=1)
            both = lax.dot_general(
                weights, v_all[...].reshape(1024, 2 * HEAD), (((1,), (0,)), ((), ())), preferred_element_type=F32
            )
            total = both[:, HEAD:]
            o_all[h, t, a] = (both[:, :HEAD] / total).astype(BF16).reshape(2, HEAD, HEAD)
            level = top + jnp.log2(total)
            for r in range(2):
                l_all[h, t, a, r:r + 1, :] = jnp.sum(
                    jnp.where(eye, level[r * HEAD:(r + 1) * HEAD], 0.0), axis=0, keepdims=True
                )

        @pl.when(t > 0)
        def _():
            for a in range(2):
                to = second_peer(a, t)
                remote(o_all.at[h, t, a], o_in.at[h, 4 - t, a], (osn.at[h], orc.at[h]), to).start()
                remote(l_all.at[h, t, a], l_in.at[h, 4 - t, a], (lsn.at[h], lrc.at[h]), to).start()

    loop(0, 8, chunk)

    def join_second(h):
        arrived(o_in.at[h, pl.ds(1, 3)], (osn.at[h], orc.at[h]))
        arrived(l_in.at[h, pl.ds(1, 3)], (lsn.at[h], lrc.at[h]))

        def block(i):
            a, k = i % 2, 1 - i // 2
            levels = [l_all[h, 0, a, pl.ds(k, 1), :]] + [l_in[h, t, a, pl.ds(k, 1), :] for t in range(1, 4)]
            level, shares = combine(levels)
            values = [o_all[h, 0, a, k]] + [o_in[h, t, a, k] for t in range(1, 4)]
            joined = weighted([expand(share) for share in shares], values).astype(BF16)
            lp_out[h, a, k] = level
            for m in range(2):
                sub = 2 * k + m
                p_out[h, sub, a] = joined[64 * m:64 * m + 64]

                @pl.when(sub > 0)
                def _():
                    to = first_peer(a, sub)
                    remote(p_out.at[h, sub, a], p_in.at[h, 4 - sub, a], (ps.at[h, 0], ps.at[h, 1]), to).start()
                    remote(lp_out.at[h, a, k], lp_in.at[h, 4 - sub, a], (lps.at[h, 0], lps.at[h, 1]), to).start()

        loop(0, 4, block)

    loop(0, 2, join_second)

    def z_part(ref, s):
        return ref.at[pl.ds(pl.multiple_of(16 * s, 16), 16)]

    low = lax.broadcasted_iota(jnp.int32, (1, HEAD), 1) < 64

    def join_first(h):
        arrived(p_in.at[h, pl.ds(1, 3)], (ps.at[h, 0], ps.at[h, 1]))
        arrived(lp_in.at[h, pl.ds(1, 3)], (lps.at[h, 0], lps.at[h, 1]))
        levels = [jnp.where(low, lp_out[h, 0, 0], pltpu.roll(lp_out[h, 1, 0], 64, 1))]
        levels.append(jnp.where(low, pltpu.roll(lp_in[h, 1, 0], 64, 1), lp_in[h, 1, 1]))
        levels.append(jnp.where(low, lp_in[h, 2, 0], pltpu.roll(lp_in[h, 2, 1], 64, 1)))
        levels.append(jnp.where(low, pltpu.roll(lp_in[h, 3, 0], 64, 1), lp_in[h, 3, 1]))
        level, shares = combine(levels)
        values = [part.reshape(HEAD, HEAD) for part in [p_out[h, 0]] + [p_in[h, b] for b in range(1, 4)]]
        joined = weighted([expand(share) for share in shares], values).astype(BF16)
        z_out[pl.ds(pl.multiple_of(128 * h, 128), 128), :] = joined
        lz_out[h] = level

        def go(i):
            s = 8 * h + (i + 4 * h) % 8

            @pl.when(s != 4)
            def _():
                to = dev(x, y, z + s - 4, core)
                at = (20 - s) % 16
                remote(z_part(z_out, s), z_in.at[at], pair(zs), to).start()
                remote(lz_out.at[h], lz_in.at[at], pair(lzs), to).start()

        loop(0, 8, go)

    loop(0, 2, join_first)
    z_in[0] = z_out[64:80, :]
    lz_in[0] = lz_out[0]
    arrived(z_in.at[pl.ds(1, 15)], pair(zs))
    arrived(lz_in.at[pl.ds(1, 15)], pair(lzs))
    lane16 = lax.broadcasted_iota(jnp.int32, (16, HEAD), 1) - lax.broadcasted_iota(jnp.int32, (16, HEAD), 0)

    def join_z(w):
        levels, values = [], []
        for m in range(4):
            at = w + 4 * m
            offset = ((20 - at) % 8) * 16
            wide = jnp.broadcast_to(lz_in[at], (16, HEAD))
            levels.append(jnp.sum(jnp.where(lane16 == offset, wide, 0.0), axis=1, keepdims=True))
            values.append(z_in[at])
        _, shares = combine(levels)
        joined = weighted(shares, values)
        f_in[2 * ((u + w) % 4) + core] = joined[:8]
        s_out[w] = joined[8:]

    loop(0, 4, join_z)
    remote(s_out, s_in, pair(fs), other).start()
    arrived(s_in, pair(fs))

    def place(w):
        f_in[2 * ((u + w) % 4) + 1 - core] = s_in[w]

    loop(0, 4, place)

    def give(c):
        for g in range(4):
            at = pl.multiple_of((4 * c + g) * HEAD, HEAD)
            out_ref[:, pl.ds(at, HEAD)] = f_in[c, 2 * g:2 * g + 2, :].astype(BF16)

    loop(0, 8, give)

    sent(q_own.at[1], pair(swap))
    sent(q_z.at[pl.ds(0, 128)], pair(s1))
    sent(z_rows(9, 7), pair(s2))
    sent(k_all.at[pl.ds(1, 7)], (kv.at[0], kv.at[1]))
    sent(v_all.at[pl.ds(1, 7), :, pl.ds(0, HEAD)], (kv.at[2], kv.at[3]))
    for h in range(2):
        sent(q_all.at[h, 0, :, pl.ds(1, 3)], (s3.at[h], s3.at[h]))
        sent(q_all.at[h, pl.ds(1, 3)], (q4s.at[h], q4r.at[h, 0]))
        sent(o_in.at[h, pl.ds(1, 3)], (osn.at[h], orc.at[h]))
        sent(l_in.at[h, pl.ds(1, 3)], (lsn.at[h], lrc.at[h]))
        sent(p_in.at[h, pl.ds(1, 3)], (ps.at[h, 0], ps.at[h, 1]))
        sent(lp_in.at[h, pl.ds(1, 3)], (lps.at[h, 0], lps.at[h, 1]))
    sent(z_in.at[pl.ds(1, 15)], pair(zs))
    sent(lz_in.at[pl.ds(1, 15)], pair(lzs))
    sent(s_in, pair(fs))


def per_device(queries, keys, values, window_blocks):
    dma = pltpu.SemaphoreType.DMA
    vmem = pltpu.VMEM
    return pl.pallas_call(
        kernel,
        out_shape=jax.ShapeDtypeStruct(queries.shape, BF16),
        in_specs=[pl.BlockSpec(memory_space=pl.ANY)] * 4,
        out_specs=pl.BlockSpec(memory_space=pltpu.VMEM),
        scratch_shapes=[
            pltpu.SMEM((16,), jnp.int32),
            vmem((2, 2, 4096), BF16), vmem((4, 16, HEAD), F32), vmem((4, 16, HEAD), BF16), vmem((256, HEAD), BF16),
            vmem((2, 4, 2, 4, 64, HEAD), BF16), vmem((8, HEAD, HEAD), BF16), vmem((8, HEAD, 2 * HEAD), BF16),
            vmem((32, HEAD), F32), vmem((32, HEAD, HEAD), F32), vmem((8, HEAD), F32),
            vmem((2, 4, 2, 2, HEAD, HEAD), BF16), vmem((2, 4, 2, 2, HEAD), F32),
            vmem((2, 4, 2, 2, HEAD, HEAD), BF16), vmem((2, 4, 2, 2, HEAD), F32),
            vmem((2, 4, 2, 64, HEAD), BF16), vmem((2, 2, 2, 1, HEAD), F32),
            vmem((2, 4, 2, 64, HEAD), BF16), vmem((2, 4, 2, 1, HEAD), F32),
            vmem((256, HEAD), BF16), vmem((2, 1, HEAD), F32),
            vmem((16, 16, HEAD), BF16), vmem((16, 1, HEAD), F32),
            vmem((4, 8, HEAD), F32), vmem((4, 8, HEAD), F32), vmem((8, 8, HEAD), F32),
            dma((4,)), dma((2,)), dma((2,)), dma((2,)), dma((2,)), dma((2, 2, 4)), dma((2,)), dma((2, 4)), dma((4,)),
            dma((2,)), dma((2,)), dma((2,)), dma((2,)), dma((2, 2)), dma((2, 2)), dma((2,)), dma((2,)), dma((2,)),
        ],
        compiler_params=pltpu.CompilerParams(
            collective_id=0, has_side_effects=True, vmem_limit_bytes=58 * 1024 * 1024
        ),
    )(queries, keys, values, window_blocks)


def solution(mesh):
    return jax.shard_map(
        per_device,
        mesh=mesh,
        in_specs=(
            P(("row", "col", "uly"), None),
            P(("col", "row", "uly"), None),
            P(("col", "row", "uly"), None),
            P(),
        ),
        out_specs=P(("row", "col", "uly"), None),
        check_vma=False,
    )
```

```python
import math

import jax
import jax.numpy as jnp
from jax import lax
from jax.experimental import pallas as pl
from jax.experimental.pallas import tpu as pltpu
from jax.sharding import PartitionSpec as P

HEAD = 128
MESH = pl.DeviceIdType.MESH
SCALE = math.log2(math.e) / math.sqrt(HEAD)
HIDDEN = -1e30
F32, BF16 = jnp.float32, jnp.bfloat16


def expand(row):
    return jnp.transpose(jnp.broadcast_to(row, (HEAD, HEAD)))


def combine(levels):
    top = jnp.maximum(jnp.maximum(levels[0], levels[1]), jnp.maximum(levels[2], levels[3]))
    shares = [jnp.exp2(level - top) for level in levels]
    inverse = 1.0 / ((shares[0] + shares[1]) + (shares[2] + shares[3]))
    return [share * inverse for share in shares]


def weighted(shares, values):
    acc = shares[0] * values[0].astype(F32)
    for share, value in zip(shares[1:], values[1:]):
        acc = acc + share * value.astype(F32)
    return acc


def kernel(
    q_ref, k_ref, v_ref, wb_ref, out_ref,
    wb, q_own, q_f32, q_cls, q_z, q_all, k_all, v_all, pos, thr, key_pos,
    o_all, l_all, o_in, l_in,
    z_out, lz_out, z_in, lz_in, s_out, s_in, f_in,
    own, swap, s1, s2, qs, qr, kv, osn, orc, lsn, lrc, zs, lzs, fs,
):
    u = lax.axis_index("uly")
    row = lax.axis_index("row")
    col = lax.axis_index("col")
    x, core = row // 2, row % 2
    y = col % 4
    z = (col // 4) * 4 + u

    def dev(x_at, y_at, z_at, core_at):
        z_at = (z_at + 16) % 16
        return {
            "uly": z_at % 4,
            "row": (x_at % 4) * 2 + core_at,
            "col": (z_at // 4) * 4 + y_at % 4,
        }

    def remote(src, dst, sems, to):
        return pltpu.make_async_remote_copy(
            src_ref=src, dst_ref=dst, send_sem=sems[0], recv_sem=sems[1], device_id=to, device_id_type=MESH
        )

    other = dev(x, y, z, 1 - core)

    def pair(sem):
        return sem.at[0], sem.at[1]

    def arrived(ref, sems):
        remote(ref, ref, sems, other).wait_recv()

    def sent(ref, sems):
        remote(ref, ref, sems, other).wait_send()

    def loop(start, stop, body):
        def step(i, carry):
            body(i)
            return carry

        lax.fori_loop(start, stop, step, 0)

    d2 = 2 - 4 * core
    barrier = pltpu.get_barrier_semaphore()

    def greet(to):
        pl.semaphore_signal(barrier, inc=1, device_id=to, device_id_type=MESH)

    def greet_z(j):
        greet(dev(x, y, z + 5 - j, core))
        greet(dev(x, y, z - 5 + j, core))

    def at_plane(n):
        return dev(x + n % 4, y + n // 4, z, core)

    def back(n):
        return (4 - n % 4) % 4 + 4 * ((4 - n // 4) % 4)

    def greet_plane(n):
        greet(at_plane(n))

    loop(1, 5, greet_z)
    loop(1, 16, greet_plane)
    greet(dev(x, y, z + 1, 1 - core))
    greet(dev(x, y, z - 1, 1 - core))
    greet(dev(x, y, z + d2, 1 - core))
    greet(other)
    own_q = pltpu.make_async_copy(q_ref, q_own.at[0], own.at[0])
    own_q.start()
    own_wb = pltpu.make_async_copy(wb_ref, wb, own.at[1])
    own_wb.start()

    def features(ref, group):
        return ref.at[:, pl.ds(pl.multiple_of(group * HEAD, HEAD), HEAD)]

    def v_place(slot):
        return v_all.at[slot, :, pl.ds(0, HEAD)]

    my_group = 2 * u + core
    own_k = pltpu.make_async_copy(features(k_ref, my_group), k_all.at[0], own.at[2])
    own_v = pltpu.make_async_copy(features(v_ref, my_group), v_place(0), own.at[3])
    own_k.start()
    own_v.start()
    v_all[:, :, HEAD:] = jnp.ones((8, HEAD, HEAD), BF16)
    pl.semaphore_wait(barrier, 27)

    remote(q_ref, q_own.at[1], pair(swap), other).start()
    own_q.wait()
    own_wb.wait()
    arrived(q_own.at[1], pair(swap))

    def pack(c):
        for r in range(2):
            for g in range(4):
                at = pl.multiple_of(((2 * c + core) * 4 + g) * HEAD, HEAD)
                q_f32[c, 8 * r + 2 * g:8 * r + 2 * g + 2, :] = q_own[r, :, pl.ds(at, HEAD)].astype(F32)
        q_cls[c] = q_f32[c].astype(BF16)

    loop(0, 4, pack)

    def z_rows(at, n):
        return q_z.at[pl.ds(pl.multiple_of(16 * at, 16), 16 * n)]

    def along_z(j):
        d = 5 - j
        remote(q_cls.at[(u + d) % 4], z_rows(4 - d, 1), pair(s1), dev(x, y, z + d, core)).start()
        remote(q_cls.at[(u - d + 4) % 4], z_rows(4 + d, 1), pair(s1), dev(x, y, z - d, core)).start()

    loop(1, 5, along_z)
    q_z[64:80, :] = q_cls[u]

    blk = lax.broadcasted_iota(jnp.int32, (32, HEAD), 0)
    lane = lax.broadcasted_iota(jnp.int32, (32, HEAD), 1)
    half, ys, xs = blk >> 4, (y + (blk >> 2)) & 3, (x + blk) & 3
    cs = jnp.where((lane & 8) == 0, core, 1 - core)
    z_src = (z + 8 * half + (lane >> 4) + 12) & 15
    which = 2 * (2 * xs + cs) + (z_src >> 3)
    block_at = jnp.zeros((32, HEAD), jnp.int32)
    for i in range(16):
        block_at = jnp.where(which == i, wb[i], block_at)
    within = (((z_src >> 2) & 1) * 4 + ys) * 8 + (z_src & 3) * 2 + (lane & 1)
    pos[...] = (64 * block_at + within).astype(F32)
    lane_f = lax.broadcasted_iota(jnp.int32, (1, HEAD), 1).astype(F32)
    sources = [(z, core), (z, 1 - core), (z - 1, 0), (z - 1, 1), (z + 1, 0), (z + 1, 1), (z - 2, 0), (z + 2, 1)]
    for j, (zt, c) in enumerate(sources):
        zt = (zt + 16) % 16
        base = (zt // 4) * 16384 + y * 4096 + x * 1024 + c * 512 + (zt % 4) * 128
        key_pos[j:j + 1, :] = lane_f + base.astype(F32)

    def spread_pos(b):
        thr[b] = expand(pos[pl.ds(b, 1), :])

    def turn(j):
        return j + j // 2 - 2 * (j // 3)

    def gather(h):
        def go(j):
            n = 4 * ((4 - turn(j // 4)) % 4) + j % 4
            there = back(n)
            to = (qs.at[h], qr.at[h, there // 4])
            remote(q_z.at[pl.ds(128 * h, 128)], q_all.at[h, there], to, at_plane(n)).start()

        loop(1, 16, go)
        q_all[h, 0] = q_z[128 * h:128 * h + 128, :]

    arrived(q_z.at[pl.ds(0, 128)], pair(s1))
    remote(z_rows(5, 4), z_rows(9, 4), pair(s2), dev(x, y, z - 4, core)).start()
    remote(z_rows(1, 3), z_rows(13, 3), pair(s2), dev(x, y, z + 4, core)).start()
    gather(0)

    def spread(group, slot, to):
        remote(features(k_ref, group), k_all.at[slot], (kv.at[0], kv.at[1]), to).start()
        remote(features(v_ref, group), v_place(slot), (kv.at[2], kv.at[3]), to).start()

    def spread_z(c):
        for d, slot in ((1, 2 + core), (-1, 4 + core), (d2, 6 + core)):
            spread(2 * ((u + d + 4) % 4) + c, slot, dev(x, y, z + d, c))

    loop(0, 2, spread_z)
    spread(2 * u + 1 - core, 1, other)

    loop(0, 32, spread_pos)
    arrived(z_rows(9, 7), pair(s2))
    gather(1)

    own_k.wait()
    own_v.wait()
    arrived(k_all.at[pl.ds(1, 7)], (kv.at[0], kv.at[1]))
    arrived(v_all.at[pl.ds(1, 7), :, pl.ds(0, HEAD)], (kv.at[2], kv.at[3]))

    eye = lax.broadcasted_iota(jnp.int32, (HEAD, HEAD), 0) == lax.broadcasted_iota(jnp.int32, (HEAD, HEAD), 1)

    def chunk(i):
        h, t = i // 4, turn(i % 4)

        @pl.when(t == 0)
        def _():
            arrived(q_all.at[h, pl.ds(1, 3)], (qs.at[h], qr.at[h, 0]))

        @pl.when(t > 0)
        def _():
            arrived(q_all.at[h, pl.ds(4 * t, 4)], (qs.at[h], qr.at[h, t]))

        for a in range(2):
            n = 4 * t + 2 * a
            q = q_all[h, pl.ds(n, 2)].reshape(256, HEAD)
            scores = lax.dot_general(
                q, k_all[...].reshape(1024, HEAD), (((1,), (1,)), ((), ())), preferred_element_type=F32
            )
            limit = thr[pl.ds(16 * h + n, 2)].reshape(256, HEAD)
            parts = [
                jnp.where(key_pos[j:j + 1, :] <= limit, scores[:, j * HEAD:(j + 1) * HEAD], HIDDEN) for j in range(8)
            ]
            top = parts[0]
            for part in parts[1:]:
                top = jnp.maximum(top, part)
            top = jnp.max(top, axis=1, keepdims=True) * SCALE
            weights = jnp.concatenate([jnp.exp2(part * SCALE - top).astype(BF16) for part in parts], axis=1)
            both = lax.dot_general(
                weights, v_all[...].reshape(1024, 2 * HEAD), (((1,), (0,)), ((), ())), preferred_element_type=F32
            )
            total = both[:, HEAD:]
            o_all[h, pl.ds(n, 2)] = (both[:, :HEAD] / total).astype(BF16).reshape(2, HEAD, HEAD)
            level = top + jnp.log2(total)
            for r in range(2):
                l_all[h, n + r] = jnp.sum(
                    jnp.where(eye, level[r * HEAD:(r + 1) * HEAD], 0.0), axis=0, keepdims=True
                )

        def go(m):
            n = 4 * t + m

            @pl.when(n > 0)
            def _():
                to = at_plane(n)
                remote(o_all.at[h, n], o_in.at[h, back(n)], (osn.at[h], orc.at[h]), to).start()
                remote(l_all.at[h, n], l_in.at[h, back(n)], (lsn.at[h], lrc.at[h]), to).start()

        loop(0, 4, go)

    loop(0, 8, chunk)

    def z_part(ref, s):
        return ref.at[pl.ds(pl.multiple_of(16 * s, 16), 16)]

    def join(h):
        o_in[h, 0] = o_all[h, 0]
        l_in[h, 0] = l_all[h, 0]
        arrived(l_in.at[h, pl.ds(1, 15)], (lsn.at[h], lrc.at[h]))
        top = l_in[h, 0]
        for n in range(1, 16):
            top = jnp.maximum(top, l_in[h, n])
        total = jnp.exp2(l_in[h, 0] - top)
        for n in range(1, 16):
            total = total + jnp.exp2(l_in[h, n] - top)
        level = top + jnp.log2(total)
        lz_out[h] = level
        arrived(o_in.at[h, pl.ds(1, 15)], (osn.at[h], orc.at[h]))

        def add(i, acc):
            for m in range(4):
                n = 4 * i + m
                acc = acc + expand(jnp.exp2(l_in[h, n] - level)) * o_in[h, n].astype(F32)
            return acc

        joined = lax.fori_loop(0, 4, add, jnp.zeros((HEAD, HEAD), F32))
        z_out[pl.ds(pl.multiple_of(128 * h, 128), 128), :] = joined.astype(BF16)

        def go(i):
            s = 8 * h + (i + 4 * h) % 8

            @pl.when(s != 4)
            def _():
                to = dev(x, y, z + s - 4, core)
                at = (20 - s) % 16
                remote(z_part(z_out, s), z_in.at[at], pair(zs), to).start()
                remote(lz_out.at[h], lz_in.at[at], pair(lzs), to).start()

        loop(0, 8, go)

    loop(0, 2, join)
    z_in[0] = z_out[64:80, :]
    lz_in[0] = lz_out[0]
    arrived(z_in.at[pl.ds(1, 15)], pair(zs))
    arrived(lz_in.at[pl.ds(1, 15)], pair(lzs))
    lane16 = lax.broadcasted_iota(jnp.int32, (16, HEAD), 1) - lax.broadcasted_iota(jnp.int32, (16, HEAD), 0)

    def join_z(w):
        levels, values = [], []
        for m in range(4):
            at = w + 4 * m
            offset = ((20 - at) % 8) * 16
            wide = jnp.broadcast_to(lz_in[at], (16, HEAD))
            levels.append(jnp.sum(jnp.where(lane16 == offset, wide, 0.0), axis=1, keepdims=True))
            values.append(z_in[at])
        shares = combine(levels)
        joined = weighted(shares, values)
        f_in[2 * ((u + w) % 4) + core] = joined[:8]
        s_out[w] = joined[8:]

    loop(0, 4, join_z)
    remote(s_out, s_in, pair(fs), other).start()
    arrived(s_in, pair(fs))

    def place(w):
        f_in[2 * ((u + w) % 4) + 1 - core] = s_in[w]

    loop(0, 4, place)

    def give(c):
        for g in range(4):
            at = pl.multiple_of((4 * c + g) * HEAD, HEAD)
            out_ref[:, pl.ds(at, HEAD)] = f_in[c, 2 * g:2 * g + 2, :].astype(BF16)

    loop(0, 8, give)

    sent(q_own.at[1], pair(swap))
    sent(q_z.at[pl.ds(0, 128)], pair(s1))
    sent(z_rows(9, 7), pair(s2))
    sent(k_all.at[pl.ds(1, 7)], (kv.at[0], kv.at[1]))
    sent(v_all.at[pl.ds(1, 7), :, pl.ds(0, HEAD)], (kv.at[2], kv.at[3]))
    for h in range(2):
        sent(q_all.at[h, pl.ds(1, 15)], (qs.at[h], qr.at[h, 0]))
        sent(o_in.at[h, pl.ds(1, 15)], (osn.at[h], orc.at[h]))
        sent(l_in.at[h, pl.ds(1, 15)], (lsn.at[h], lrc.at[h]))
    sent(z_in.at[pl.ds(1, 15)], pair(zs))
    sent(lz_in.at[pl.ds(1, 15)], pair(lzs))
    sent(s_in, pair(fs))


def per_device(queries, keys, values, window_blocks):
    dma = pltpu.SemaphoreType.DMA
    vmem = pltpu.VMEM
    return pl.pallas_call(
        kernel,
        out_shape=jax.ShapeDtypeStruct(queries.shape, BF16),
        in_specs=[pl.BlockSpec(memory_space=pl.ANY)] * 4,
        out_specs=pl.BlockSpec(memory_space=pltpu.VMEM),
        scratch_shapes=[
            pltpu.SMEM((16,), jnp.int32),
            vmem((2, 2, 4096), BF16), vmem((4, 16, HEAD), F32), vmem((4, 16, HEAD), BF16), vmem((256, HEAD), BF16),
            vmem((2, 16, HEAD, HEAD), BF16), vmem((8, HEAD, HEAD), BF16), vmem((8, HEAD, 2 * HEAD), BF16),
            vmem((32, HEAD), F32), vmem((32, HEAD, HEAD), F32), vmem((8, HEAD), F32),
            vmem((2, 16, HEAD, HEAD), BF16), vmem((2, 16, 1, HEAD), F32),
            vmem((2, 16, HEAD, HEAD), BF16), vmem((2, 16, 1, HEAD), F32),
            vmem((256, HEAD), BF16), vmem((2, 1, HEAD), F32),
            vmem((16, 16, HEAD), BF16), vmem((16, 1, HEAD), F32),
            vmem((4, 8, HEAD), F32), vmem((4, 8, HEAD), F32), vmem((8, 8, HEAD), F32),
            dma((4,)), dma((2,)), dma((2,)), dma((2,)), dma((2,)), dma((2, 4)), dma((4,)),
            dma((2,)), dma((2,)), dma((2,)), dma((2,)), dma((2,)), dma((2,)), dma((2,)),
        ],
        compiler_params=pltpu.CompilerParams(
            collective_id=0, has_side_effects=True, vmem_limit_bytes=58 * 1024 * 1024
        ),
    )(queries, keys, values, window_blocks)


def solution(mesh):
    return jax.shard_map(
        per_device,
        mesh=mesh,
        in_specs=(
            P(("row", "col", "uly"), None),
            P(("col", "row", "uly"), None),
            P(("col", "row", "uly"), None),
            P(),
        ),
        out_specs=P(("row", "col", "uly"), None),
        check_vma=False,
    )
```

```python
import math

import jax
import jax.numpy as jnp
from jax import lax
from jax.experimental import pallas as pl
from jax.experimental.pallas import tpu as pltpu
from jax.sharding import PartitionSpec as P

HEAD = 128
MESH = pl.DeviceIdType.MESH
SCALE = math.log2(math.e) / math.sqrt(HEAD)
HIDDEN = -1e30
F32, BF16 = jnp.float32, jnp.bfloat16


def expand(row):
    return jnp.transpose(jnp.broadcast_to(row, (HEAD, HEAD)))


def combine(levels):
    top = jnp.maximum(jnp.maximum(levels[0], levels[1]), jnp.maximum(levels[2], levels[3]))
    shares = [jnp.exp2(level - top) for level in levels]
    total = (shares[0] + shares[1]) + (shares[2] + shares[3])
    inverse = 1.0 / total
    return top + jnp.log2(total), [share * inverse for share in shares]


def weighted(shares, values):
    acc = shares[0] * values[0].astype(F32)
    for share, value in zip(shares[1:], values[1:]):
        acc = acc + share * value.astype(F32)
    return acc


def kernel(
    q_ref, k_ref, v_ref, wb_ref, out_ref,
    wb, q_own, q_f32, q_cls, q_z, q_all, k_all, v_all, pos, thr, key_pos,
    o_all, l_all, o_in, l_in, p_out, lp_out, p_in, lp_in, ob_in, lb_in, share_b,
    z_out, lz_out, z_in, lz_in, s_out, s_in, f_in,
    own, swap, s1, s2, s3, s3r, q4s, q4r, kv, os, ls, ps, lps, obs, lbs, zs, lzs, fs,
):
    u = lax.axis_index("uly")
    row = lax.axis_index("row")
    col = lax.axis_index("col")
    rem, div = lax.rem, lax.div
    x, core = div(row, 2), rem(row, 2)
    y, z_high = rem(col, 4), div(col, 4)
    z = z_high * 4 + u

    def along(d, core_at):
        z_at = rem(z + (d + 16), 16)
        return {"uly": rem(z_at, 4), "row": 2 * x + core_at, "col": div(z_at, 4) * 4 + y}

    def plane(dx, dy):
        return {"uly": u, "row": 2 * rem(x + dx, 4) + core, "col": 4 * z_high + rem(y + dy, 4)}

    def remote(src, dst, sems, to):
        return pltpu.make_async_remote_copy(
            src_ref=src, dst_ref=dst, send_sem=sems[0], recv_sem=sems[1], device_id=to, device_id_type=MESH
        )

    other = {"uly": u, "row": 2 * x + 1 - core, "col": col}

    def pair(sem):
        return sem.at[0], sem.at[1]

    def arrived(ref, sems):
        remote(ref, ref, sems, other).wait_recv()

    def sent(ref, sems):
        remote(ref, ref, sems, other).wait_send()

    def loop(start, stop, body):
        def step(i, carry):
            body(i)
            return carry

        lax.fori_loop(start, stop, step, 0)

    d2 = 2 - 4 * core
    barrier = pltpu.get_barrier_semaphore()

    def greet(to):
        pl.semaphore_signal(barrier, inc=1, device_id=to, device_id_type=MESH)

    for d in (4, -4, 3, -3, 2, -2, 1, -1):
        greet(along(d, core))
    for i in (2, 1, 3):
        greet(plane(i, 0))
        greet(plane(0, i))
    for d in (d2, 1, -1):
        greet(along(d, 1 - core))
    greet(other)
    own_q = pltpu.make_async_copy(q_ref, q_own.at[0], own.at[0])
    own_q.start()
    own_wb = pltpu.make_async_copy(wb_ref, wb, own.at[1])
    own_wb.start()

    def features(ref, group):
        return ref.at[:, pl.ds(pl.multiple_of(group * HEAD, HEAD), HEAD)]

    def v_place(slot):
        return v_all.at[slot, :, pl.ds(0, HEAD)]

    my_group = 2 * u + core
    own_k = pltpu.make_async_copy(features(k_ref, my_group), k_all.at[0], own.at[2])
    own_v = pltpu.make_async_copy(features(v_ref, my_group), v_place(0), own.at[3])
    own_k.start()
    own_v.start()
    v_all[:, :, HEAD:] = jnp.ones((8, HEAD, HEAD), BF16)
    pl.semaphore_wait(barrier, 18)

    remote(q_ref, q_own.at[1], pair(swap), other).start()
    own_q.wait()
    own_wb.wait()
    arrived(q_own.at[1], pair(swap))

    def pack(c):
        for r in range(2):
            for g in range(4):
                at = pl.multiple_of(((2 * c + core) * 4 + g) * HEAD, HEAD)
                q_f32[c, 8 * r + 2 * g:8 * r + 2 * g + 2, :] = q_own[r, :, pl.ds(at, HEAD)].astype(F32)
        q_cls[c] = q_f32[c].astype(BF16)

    loop(0, 4, pack)

    def z_rows(at, n):
        return q_z.at[pl.ds(pl.multiple_of(16 * at, 16), 16 * n)]

    for d in (4, -4, 3, -3, 2, -2, 1, -1):
        remote(q_cls.at[rem(u + d + 4, 4)], z_rows(4 - d, 1), pair(s1), along(d, core)).start()
    q_z[64:80, :] = q_cls[u]

    def spread(what):
        def one(group, slot, to):
            src = features(v_ref if what else k_ref, group)
            dst = v_place(slot) if what else k_all.at[slot]
            remote(src, dst, (kv.at[2 * what], kv.at[2 * what + 1]), to).start()

        for d, slot in ((d2, 6 + core), (1, 2 + core), (-1, 4 + core)):
            for c in range(2):
                one(2 * rem(u + d + 4, 4) + c, slot, along(d, c))
        one(2 * u + 1 - core, 1, other)

    spread(0)

    blk = lax.broadcasted_iota(jnp.int32, (32, HEAD), 0)
    lane = lax.broadcasted_iota(jnp.int32, (32, HEAD), 1)
    half, step, side, sub = blk >> 4, (blk >> 2) & 3, (blk >> 1) & 1, 2 * (blk & 1) + (lane >> 6)
    ys = (y + jnp.where(side == 0, step, sub)) & 3
    xs = (x + jnp.where(side == 0, sub, step)) & 3
    cs = jnp.where((lane & 8) == 0, core, 1 - core)
    z_src = (z + 8 * half + 4 * side + ((lane >> 4) & 3) + 12) & 15
    which = 2 * (2 * xs + cs) + (z_src >> 3)
    block_at = jnp.zeros((32, HEAD), jnp.int32)
    for i in range(16):
        block_at = jnp.where(which == i, wb[i], block_at)
    within = (((z_src >> 2) & 1) * 4 + ys) * 8 + (z_src & 3) * 2 + (lane & 1)
    pos[...] = (64 * block_at + within).astype(F32)
    lane_f = lax.broadcasted_iota(jnp.int32, (1, HEAD), 1).astype(F32)
    sources = [(z, core), (z, 1 - core), (z - 1, 0), (z - 1, 1), (z + 1, 0), (z + 1, 1), (z - 2, 0), (z + 2, 1)]
    for j, (zt, c) in enumerate(sources):
        zt = rem(zt + 16, 16)
        base = div(zt, 4) * 16384 + y * 4096 + x * 1024 + c * 512 + rem(zt, 4) * 128
        key_pos[j:j + 1, :] = lane_f + base.astype(F32)

    def spread_pos(b):
        thr[b] = expand(pos[pl.ds(b, 1), :])

    def first_peer(a, i):
        return plane(0, i) if a else plane(i, 0)

    def second_peer(a, i):
        return plane(i, 0) if a else plane(0, i)

    def first(h):
        for a in range(2):
            mine = q_z.at[pl.ds(128 * h + 64 * a, 64)]

            def go(i):
                remote(mine, q_all.at[h, 0, a, 4 - i], (s3.at[h], s3r.at[h, a, 4 - i]), first_peer(a, i)).start()

            loop(1, 4, go)
        for a in range(2):
            mine = q_z.at[pl.ds(128 * h + 64 * a, 64)]

            def go_on(i):
                remote(mine, q_all.at[h, 4 - i, a, 0], (q4s.at[h], q4r.at[h, 4 - i]), second_peer(a, i)).start()

            loop(1, 4, go_on)
            q_all[h, 0, a, 0] = q_z[128 * h + 64 * a:128 * h + 64 * a + 64, :]

    def second(h):
        def pass_on(j):
            r = j + div(j, 2) - 2 * div(j, 3)
            for a in range(2):
                block = q_all.at[h, 0, a, r]
                arrived(block, (s3.at[h], s3r.at[h, a, r]))

                def go(i):
                    remote(block, q_all.at[h, 4 - i, a, r], (q4s.at[h], q4r.at[h, 4 - i]), second_peer(a, i)).start()

                loop(1, 4, go)

        loop(1, 4, pass_on)

    arrived(q_z.at[pl.ds(0, 128)], pair(s1))
    remote(z_rows(5, 4), z_rows(9, 4), pair(s2), along(-4, core)).start()
    remote(z_rows(1, 3), z_rows(13, 3), pair(s2), along(4, core)).start()
    first(0)

    spread(1)
    loop(0, 32, spread_pos)
    second(0)
    arrived(z_rows(9, 7), pair(s2))
    first(1)

    own_k.wait()
    own_v.wait()
    arrived(k_all.at[pl.ds(1, 7)], (kv.at[0], kv.at[1]))
    arrived(v_all.at[pl.ds(1, 7), :, pl.ds(0, HEAD)], (kv.at[2], kv.at[3]))

    eye = lax.broadcasted_iota(jnp.int32, (HEAD, HEAD), 0) == lax.broadcasted_iota(jnp.int32, (HEAD, HEAD), 1)

    def chunk(i):
        code = i - (div(i + 6, 8) - div(i + 3, 8)) + 3 * (div(i + 7, 8) - div(i + 6, 8))
        h, t = div(code, 4), rem(code, 4)

        @pl.when(i == 1)
        def _():
            second(1)

        @pl.when(t > 0)
        def _():
            arrived(q_all.at[h, t], (q4s.at[h], q4r.at[h, t]))

        for a in range(2):
            q = q_all[h, t, a].reshape(256, HEAD)
            scores = lax.dot_general(
                q, k_all[...].reshape(1024, HEAD), (((1,), (1,)), ((), ())), preferred_element_type=F32
            )
            limit = thr[pl.ds(4 * code + 2 * a, 2)].reshape(256, HEAD)
            parts = [
                jnp.where(key_pos[j:j + 1, :] <= limit, scores[:, j * HEAD:(j + 1) * HEAD], HIDDEN) for j in range(8)
            ]
            top = parts[0]
            for part in parts[1:]:
                top = jnp.maximum(top, part)
            top = jnp.max(top, axis=1, keepdims=True) * SCALE
            weights = jnp.concatenate([jnp.exp2(part * SCALE - top).astype(BF16) for part in parts], axis=1)
            both = lax.dot_general(
                weights, v_all[...].reshape(1024, 2 * HEAD), (((1,), (0,)), ((), ())), preferred_element_type=F32
            )
            total = both[:, HEAD:]
            o_all[h, t, a] = (both[:, :HEAD] / total).astype(BF16).reshape(2, HEAD, HEAD)
            level = top + jnp.log2(total)
            for r in range(2):
                l_all[h, t, a, r] = jnp.sum(
                    jnp.where(eye, level[r * HEAD:(r + 1) * HEAD], 0.0), axis=0, keepdims=True
                )

        @pl.when((t > 0) & (h == 0))
        def _():
            for a in range(2):
                to = second_peer(a, t)
                remote(o_all.at[0, t, a], o_in.at[4 - t, a], pair(os), to).start()
                remote(l_all.at[0, t, a], l_in.at[4 - t, a], pair(ls), to).start()

        @pl.when(h == 1)
        def _():
            for a in range(2):
                for sub in range(4):

                    @pl.when((t > 0) | (sub > 0))
                    def _():
                        back_t, back_sub = rem(4 - t, 4), (4 - sub) % 4
                        to = plane(t, sub) if a else plane(sub, t)
                        there = 4 * back_sub + back_t if a else 4 * back_t + back_sub
                        part = o_all.at[1, t, a, sub // 2, pl.ds(64 * (sub % 2), 64)]
                        remote(part, ob_in.at[there, pl.ds(64 * a, 64)], pair(obs), to).start()
                        remote(l_all.at[1, t, a, sub // 2], lb_in.at[there, a], pair(lbs), to).start()

    loop(0, 8, chunk)

    def z_part(ref, s):
        return ref.at[pl.ds(pl.multiple_of(16 * s, 16), 16)]

    def send_home(h, joined, level):
        z_out[128 * h:128 * h + 128, :] = joined.astype(BF16)
        lz_out[h] = level

        def go(i):
            s = 8 * h + rem(i + 4 * h, 8)

            @pl.when(s != 4)
            def _():
                to = along(s - 4, core)
                at = rem(20 - s, 16)
                remote(z_part(z_out, s), z_in.at[at], pair(zs), to).start()
                remote(lz_out.at[h], lz_in.at[at], pair(lzs), to).start()

        loop(0, 8, go)

    low = lax.broadcasted_iota(jnp.int32, (1, HEAD), 1) < 64

    def level_of(lower, lower_odd, upper, upper_odd):
        lower = pltpu.roll(lower, 64, 1) if lower_odd else lower
        upper = upper if upper_odd else pltpu.roll(upper, 64, 1)
        return jnp.where(low, lower, upper)

    def join_second():
        arrived(o_in.at[pl.ds(1, 3)], pair(os))
        arrived(l_in.at[pl.ds(1, 3)], pair(ls))

        def block(a, k):
            levels = [l_all[0, 0, a, k]] + [l_in[t, a, k] for t in range(1, 4)]
            level, shares = combine(levels)
            values = [o_all[0, 0, a, k]] + [o_in[t, a, k] for t in range(1, 4)]
            joined = weighted([expand(share) for share in shares], values).astype(BF16)
            lp_out[a, k] = level
            for m in range(2):
                sub = 2 * k + m
                p_out[sub, a] = joined[64 * m:64 * m + 64]

                @pl.when(sub > 0)
                def _():
                    to = first_peer(a, sub)
                    remote(p_out.at[sub, a], p_in.at[4 - sub, a], pair(ps), to).start()
                    remote(lp_out.at[a, k], lp_in.at[4 - sub, a], pair(lps), to).start()

        for a in range(2):
            loop(0, 2, lambda i, a=a: block(a, 1 - i))

    def join_first():
        arrived(p_in.at[pl.ds(1, 3)], pair(ps))
        arrived(lp_in.at[pl.ds(1, 3)], pair(lps))
        levels = [level_of(lp_out[0, 0], 0, lp_out[1, 0], 0)]
        levels += [level_of(lp_in[r, 0], r % 2, lp_in[r, 1], r % 2) for r in range(1, 4)]
        level, shares = combine(levels)
        values = [part.reshape(HEAD, HEAD) for part in [p_out[0]] + [p_in[r] for r in range(1, 4)]]
        send_home(0, weighted([expand(share) for share in shares], values), level)

    def join_plane():
        for a in range(2):
            ob_in[0, 64 * a:64 * a + 64, :] = o_all[1, 0, a, 0, 0:64, :]
            lb_in[0, a] = l_all[1, 0, a, 0]
        arrived(lb_in.at[pl.ds(1, 15)], pair(lbs))
        levels = [level_of(lb_in[n, 0], n % 2, lb_in[n, 1], (n // 4) % 2) for n in range(16)]
        top = levels[0]
        for level in levels[1:]:
            top = jnp.maximum(top, level)
        total = jnp.exp2(levels[0] - top)
        for level in levels[1:]:
            total = total + jnp.exp2(level - top)
        whole = top + jnp.log2(total)
        for n in range(16):
            share_b[n] = jnp.exp2(levels[n] - whole)
        arrived(ob_in.at[pl.ds(1, 15)], pair(obs))

        def add(i, acc):
            for m in range(4):
                acc = acc + expand(share_b[4 * i + m]) * ob_in[4 * i + m].astype(F32)
            return acc

        send_home(1, lax.fori_loop(0, 4, add, jnp.zeros((HEAD, HEAD), F32)), whole)

    join_second()
    join_first()
    join_plane()
    z_in[0] = z_out[64:80, :]
    lz_in[0] = lz_out[0]
    arrived(z_in.at[pl.ds(1, 15)], pair(zs))
    arrived(lz_in.at[pl.ds(1, 15)], pair(lzs))
    lane16 = lax.broadcasted_iota(jnp.int32, (16, HEAD), 1) - lax.broadcasted_iota(jnp.int32, (16, HEAD), 0)

    def join_z(w):
        levels, values = [], []
        for m in range(4):
            at = w + 4 * m
            offset = rem(20 - at, 8) * 16
            wide = jnp.broadcast_to(lz_in[at], (16, HEAD))
            levels.append(jnp.sum(jnp.where(lane16 == offset, wide, 0.0), axis=1, keepdims=True))
            values.append(z_in[at])
        _, shares = combine(levels)
        joined = weighted(shares, values)
        f_in[2 * rem(u + w, 4) + core] = joined[:8]
        s_out[w] = joined[8:]

    loop(0, 4, join_z)
    remote(s_out, s_in, pair(fs), other).start()
    arrived(s_in, pair(fs))

    def place(w):
        f_in[2 * rem(u + w, 4) + 1 - core] = s_in[w]

    loop(0, 4, place)

    def give(c):
        for g in range(4):
            at = pl.multiple_of((4 * c + g) * HEAD, HEAD)
            out_ref[:, pl.ds(at, HEAD)] = f_in[c, 2 * g:2 * g + 2, :].astype(BF16)

    loop(0, 8, give)

    sent(q_own.at[1], pair(swap))
    sent(q_z.at[pl.ds(0, 128)], pair(s1))
    sent(z_rows(9, 7), pair(s2))
    sent(k_all.at[pl.ds(1, 7)], (kv.at[0], kv.at[1]))
    sent(v_all.at[pl.ds(1, 7), :, pl.ds(0, HEAD)], (kv.at[2], kv.at[3]))
    for h in range(2):
        sent(q_all.at[h, 0, :, pl.ds(1, 3)], (s3.at[h], s3.at[h]))
        sent(q_all.at[h, pl.ds(1, 3)], (q4s.at[h], q4r.at[h, 0]))
    sent(o_in.at[pl.ds(1, 3)], pair(os))
    sent(l_in.at[pl.ds(1, 3)], pair(ls))
    sent(p_in.at[pl.ds(1, 3)], pair(ps))
    sent(lp_in.at[pl.ds(1, 3)], pair(lps))
    sent(ob_in.at[pl.ds(1, 15)], pair(obs))
    sent(lb_in.at[pl.ds(1, 15)], pair(lbs))
    sent(z_in.at[pl.ds(1, 15)], pair(zs))
    sent(lz_in.at[pl.ds(1, 15)], pair(lzs))
    sent(s_in, pair(fs))


def per_device(queries, keys, values, window_blocks):
    dma = pltpu.SemaphoreType.DMA
    vmem = pltpu.VMEM
    return pl.pallas_call(
        kernel,
        out_shape=jax.ShapeDtypeStruct(queries.shape, BF16),
        in_specs=[pl.BlockSpec(memory_space=pl.ANY)] * 4,
        out_specs=pl.BlockSpec(memory_space=pltpu.VMEM),
        scratch_shapes=[
            pltpu.SMEM((16,), jnp.int32),
            vmem((2, 2, 4096), BF16), vmem((4, 16, HEAD), F32), vmem((4, 16, HEAD), BF16), vmem((256, HEAD), BF16),
            vmem((2, 4, 2, 4, 64, HEAD), BF16), vmem((8, HEAD, HEAD), BF16), vmem((8, HEAD, 2 * HEAD), BF16),
            vmem((32, HEAD), F32), vmem((32, HEAD, HEAD), F32), vmem((8, HEAD), F32),
            vmem((2, 4, 2, 2, HEAD, HEAD), BF16), vmem((2, 4, 2, 2, 1, HEAD), F32),
            vmem((4, 2, 2, HEAD, HEAD), BF16), vmem((4, 2, 2, 1, HEAD), F32),
            vmem((4, 2, 64, HEAD), BF16), vmem((2, 2, 1, HEAD), F32),
            vmem((4, 2, 64, HEAD), BF16), vmem((4, 2, 1, HEAD), F32),
            vmem((16, HEAD, HEAD), BF16), vmem((16, 2, 1, HEAD), F32), vmem((16, 1, HEAD), F32),
            vmem((256, HEAD), BF16), vmem((2, 1, HEAD), F32),
            vmem((16, 16, HEAD), BF16), vmem((16, 1, HEAD), F32),
            vmem((4, 8, HEAD), F32), vmem((4, 8, HEAD), F32), vmem((8, 8, HEAD), F32),
            dma((4,)), dma((2,)), dma((2,)), dma((2,)), dma((2,)), dma((2, 2, 4)), dma((2,)), dma((2, 4)), dma((4,)),
            dma((2,)), dma((2,)), dma((2,)), dma((2,)), dma((2,)), dma((2,)), dma((2,)), dma((2,)), dma((2,)),
        ],
        compiler_params=pltpu.CompilerParams(
            collective_id=0, has_side_effects=True, vmem_limit_bytes=58 * 1024 * 1024
        ),
    )(queries, keys, values, window_blocks)


def solution(mesh):
    return jax.shard_map(
        per_device,
        mesh=mesh,
        in_specs=(
            P(("row", "col", "uly"), None),
            P(("col", "row", "uly"), None),
            P(("col", "row", "uly"), None),
            P(),
        ),
        out_specs=P(("row", "col", "uly"), None),
        check_vma=False,
    )
```

```python
import math

import jax
import jax.numpy as jnp
from jax import lax
from jax.experimental import pallas as pl
from jax.experimental.pallas import tpu as pltpu
from jax.sharding import PartitionSpec as P

HEAD = 128
MESH = pl.DeviceIdType.MESH
SCALE = 1.0 / math.sqrt(HEAD)
HIDDEN = -1e30
F32, BF16 = jnp.float32, jnp.bfloat16


def expand(row):
    return jnp.transpose(jnp.broadcast_to(row, (HEAD, HEAD)))


def combine(levels):
    top = jnp.maximum(jnp.maximum(levels[0], levels[1]), jnp.maximum(levels[2], levels[3]))
    shares = [jnp.exp(level - top) for level in levels]
    total = (shares[0] + shares[1]) + (shares[2] + shares[3])
    inverse = 1.0 / total
    return top + jnp.log(total), [share * inverse for share in shares]


def weighted(shares, values):
    acc = shares[0] * values[0].astype(F32)
    for share, value in zip(shares[1:], values[1:]):
        acc = acc + share * value.astype(F32)
    return acc


def kernel(
    q_ref, k_ref, v_ref, wb_ref, out_ref,
    wb, q_own, q_f32, q_cls, q_z, q_all, k_all, v_all, pos, thr, key_pos,
    o_all, l_all, o_in, l_in, p_out, lp_out, p_in, lp_in, ob_in, lb_in, share_b,
    z_out, lz_out, z_in, lz_in, s_out, s_in, f_in,
    own, swap, s1, s2, s3, s3r, q4s, q4r, kv, os, ls, ps, lps, obs, lbs, zs, lzs, fs,
):
    u = lax.axis_index("uly")
    row = lax.axis_index("row")
    col = lax.axis_index("col")
    rem, div = lax.rem, lax.div
    x, core = div(row, 2), rem(row, 2)
    y, z_high = rem(col, 4), div(col, 4)
    z = z_high * 4 + u

    def along(d, core_at):
        z_at = rem(z + (d + 16), 16)
        return {"uly": rem(z_at, 4), "row": 2 * x + core_at, "col": div(z_at, 4) * 4 + y}

    def plane(dx, dy):
        return {"uly": u, "row": 2 * rem(x + dx, 4) + core, "col": 4 * z_high + rem(y + dy, 4)}

    def remote(src, dst, sems, to):
        return pltpu.make_async_remote_copy(
            src_ref=src, dst_ref=dst, send_sem=sems[0], recv_sem=sems[1], device_id=to, device_id_type=MESH
        )

    other = {"uly": u, "row": 2 * x + 1 - core, "col": col}

    def pair(sem):
        return sem.at[0], sem.at[1]

    def arrived(ref, sems):
        remote(ref, ref, sems, other).wait_recv()

    def sent(ref, sems):
        remote(ref, ref, sems, other).wait_send()

    def loop(start, stop, body):
        def step(i, carry):
            body(i)
            return carry

        lax.fori_loop(start, stop, step, 0)

    d2 = 2 - 4 * core
    barrier = pltpu.get_barrier_semaphore()

    def greet(to):
        pl.semaphore_signal(barrier, inc=1, device_id=to, device_id_type=MESH)

    for d in (4, -4, 3, -3, 2, -2):
        greet(along(d, core))
    greet(plane(2, 0))
    greet(plane(0, 2))
    greet(along(d2, 1 - core))
    for d in (1, -1):
        greet(along(d, 1 - core))
        greet(along(d, core))
        greet(plane(d + 4, 0))
        greet(plane(0, d + 4))
    greet(other)
    own_q = pltpu.make_async_copy(q_ref, q_own.at[0], own.at[0])
    own_q.start()
    own_wb = pltpu.make_async_copy(wb_ref, wb, own.at[1])
    own_wb.start()

    def features(ref, group):
        return ref.at[:, pl.ds(pl.multiple_of(group * HEAD, HEAD), HEAD)]

    def v_place(slot):
        return v_all.at[slot, :, pl.ds(0, HEAD)]

    my_group = 2 * u + core
    own_k = pltpu.make_async_copy(features(k_ref, my_group), k_all.at[0], own.at[2])
    own_v = pltpu.make_async_copy(features(v_ref, my_group), v_place(0), own.at[3])
    own_k.start()
    own_v.start()
    v_all[:, :, HEAD:] = jnp.ones((8, HEAD, HEAD), BF16)
    pl.semaphore_wait(barrier, 18)

    remote(q_ref, q_own.at[1], pair(swap), other).start()
    own_q.wait()
    own_wb.wait()
    arrived(q_own.at[1], pair(swap))

    def pack(c):
        for r in range(2):
            for g in range(4):
                at = pl.multiple_of(((2 * c + core) * 4 + g) * HEAD, HEAD)
                q_f32[c, 8 * r + 2 * g:8 * r + 2 * g + 2, :] = q_own[r, :, pl.ds(at, HEAD)].astype(F32)
        q_cls[c] = q_f32[c].astype(BF16)

    loop(0, 4, pack)

    def z_rows(at, n):
        return q_z.at[pl.ds(pl.multiple_of(16 * at, 16), 16 * n)]

    for d in (4, -4, 3, -3, 2, -2, 1, -1):
        remote(q_cls.at[rem(u + d + 4, 4)], z_rows(4 - d, 1), pair(s1), along(d, core)).start()
    q_z[64:80, :] = q_cls[u]

    def spread(what):
        def one(group, slot, to):
            src = features(v_ref if what else k_ref, group)
            dst = v_place(slot) if what else k_all.at[slot]
            remote(src, dst, (kv.at[2 * what], kv.at[2 * what + 1]), to).start()

        for d, slot in ((d2, 6 + core), (1, 2 + core), (-1, 4 + core)):
            for c in range(2):
                one(2 * rem(u + d + 4, 4) + c, slot, along(d, c))
        one(2 * u + 1 - core, 1, other)

    spread(0)

    blk = lax.broadcasted_iota(jnp.int32, (32, HEAD), 0)
    lane = lax.broadcasted_iota(jnp.int32, (32, HEAD), 1)
    half, step, side, sub = blk >> 4, (blk >> 2) & 3, (blk >> 1) & 1, 2 * (blk & 1) + (lane >> 6)
    ys = (y + jnp.where(side == 0, step, sub)) & 3
    xs = (x + jnp.where(side == 0, sub, step)) & 3
    cs = jnp.where((lane & 8) == 0, core, 1 - core)
    z_src = (z + 8 * half + 4 * side + ((lane >> 4) & 3) + 12) & 15
    which = 2 * (2 * xs + cs) + (z_src >> 3)
    block_at = jnp.zeros((32, HEAD), jnp.int32)
    for i in range(16):
        block_at = jnp.where(which == i, wb[i], block_at)
    within = (((z_src >> 2) & 1) * 4 + ys) * 8 + (z_src & 3) * 2 + (lane & 1)
    pos[...] = (64 * block_at + within).astype(F32)
    lane_f = lax.broadcasted_iota(jnp.int32, (1, HEAD), 1).astype(F32)
    sources = [(z, core), (z, 1 - core), (z - 1, 0), (z - 1, 1), (z + 1, 0), (z + 1, 1), (z - 2, 0), (z + 2, 1)]
    for j, (zt, c) in enumerate(sources):
        zt = rem(zt + 16, 16)
        base = div(zt, 4) * 16384 + y * 4096 + x * 1024 + c * 512 + rem(zt, 4) * 128
        key_pos[j:j + 1, :] = lane_f + base.astype(F32)

    def spread_pos(b):
        thr[b] = expand(pos[pl.ds(b, 1), :])

    def first_peer(a, i):
        return plane(0, i) if a else plane(i, 0)

    def second_peer(a, i):
        return plane(i, 0) if a else plane(0, i)

    def first(h):
        for a in range(2):
            mine = q_z.at[pl.ds(128 * h + 64 * a, 64)]

            def go(i):
                remote(mine, q_all.at[h, 0, a, 4 - i], (s3.at[h], s3r.at[h, a, 4 - i]), first_peer(a, i)).start()

            loop(1, 4, go)
        for a in range(2):
            mine = q_z.at[pl.ds(128 * h + 64 * a, 64)]

            def go_on(i):
                remote(mine, q_all.at[h, 4 - i, a, 0], (q4s.at[h], q4r.at[h, 4 - i]), second_peer(a, i)).start()

            loop(1, 4, go_on)
            q_all[h, 0, a, 0] = q_z[128 * h + 64 * a:128 * h + 64 * a + 64, :]

    def second(h):
        def pass_on(j):
            r = j + div(j, 2) - 2 * div(j, 3)
            for a in range(2):
                block = q_all.at[h, 0, a, r]
                arrived(block, (s3.at[h], s3r.at[h, a, r]))

                def go(i):
                    remote(block, q_all.at[h, 4 - i, a, r], (q4s.at[h], q4r.at[h, 4 - i]), second_peer(a, i)).start()

                loop(1, 4, go)

        loop(1, 4, pass_on)

    arrived(q_z.at[pl.ds(0, 128)], pair(s1))
    remote(z_rows(5, 4), z_rows(9, 4), pair(s2), along(-4, core)).start()
    remote(z_rows(1, 3), z_rows(13, 3), pair(s2), along(4, core)).start()
    first(0)

    spread(1)
    loop(0, 32, spread_pos)
    second(0)
    arrived(z_rows(9, 7), pair(s2))
    first(1)

    own_k.wait()
    own_v.wait()
    arrived(k_all.at[pl.ds(1, 7)], (kv.at[0], kv.at[1]))
    arrived(v_all.at[pl.ds(1, 7), :, pl.ds(0, HEAD)], (kv.at[2], kv.at[3]))

    eye = lax.broadcasted_iota(jnp.int32, (HEAD, HEAD), 0) == lax.broadcasted_iota(jnp.int32, (HEAD, HEAD), 1)

    def chunk(i):
        code = i - (div(i + 6, 8) - div(i + 3, 8)) + 3 * (div(i + 7, 8) - div(i + 6, 8))
        h, t = div(code, 4), rem(code, 4)

        @pl.when(i == 1)
        def _():
            second(1)

        @pl.when(t > 0)
        def _():
            arrived(q_all.at[h, t], (q4s.at[h], q4r.at[h, t]))

        for a in range(2):
            q = q_all[h, t, a].reshape(256, HEAD)
            scores = lax.dot_general(
                q, k_all[...].reshape(1024, HEAD), (((1,), (1,)), ((), ())), preferred_element_type=F32
            )
            limit = thr[pl.ds(4 * code + 2 * a, 2)].reshape(256, HEAD)
            parts = [
                jnp.where(key_pos[j:j + 1, :] <= limit, scores[:, j * HEAD:(j + 1) * HEAD], HIDDEN) for j in range(8)
            ]
            top = parts[0]
            for part in parts[1:]:
                top = jnp.maximum(top, part)
            top = jnp.max(top, axis=1, keepdims=True) * SCALE
            weights = jnp.concatenate([jnp.exp(part * SCALE - top).astype(BF16) for part in parts], axis=1)
            both = lax.dot_general(
                weights, v_all[...].reshape(1024, 2 * HEAD), (((1,), (0,)), ((), ())), preferred_element_type=F32
            )
            total = both[:, HEAD:]
            o_all[h, t, a] = (both[:, :HEAD] / total).astype(BF16).reshape(2, HEAD, HEAD)
            level = top + jnp.log(total)
            for r in range(2):
                l_all[h, t, a, r] = jnp.sum(
                    jnp.where(eye, level[r * HEAD:(r + 1) * HEAD], 0.0), axis=0, keepdims=True
                )

        @pl.when((t > 0) & (h == 0))
        def _():
            for a in range(2):
                to = second_peer(a, t)
                remote(o_all.at[0, t, a], o_in.at[4 - t, a], pair(os), to).start()
                remote(l_all.at[0, t, a], l_in.at[4 - t, a], pair(ls), to).start()

        @pl.when(h == 1)
        def _():
            for a in range(2):
                for sub in range(4):

                    @pl.when((t > 0) | (sub > 0))
                    def _():
                        back_t, back_sub = rem(4 - t, 4), (4 - sub) % 4
                        to = plane(t, sub) if a else plane(sub, t)
                        there = 4 * back_sub + back_t if a else 4 * back_t + back_sub
                        part = o_all.at[1, t, a, sub // 2, pl.ds(64 * (sub % 2), 64)]
                        remote(part, ob_in.at[there, pl.ds(64 * a, 64)], pair(obs), to).start()
                        remote(l_all.at[1, t, a, sub // 2], lb_in.at[there, a], pair(lbs), to).start()

    loop(0, 8, chunk)

    def z_part(ref, s):
        return ref.at[pl.ds(pl.multiple_of(16 * s, 16), 16)]

    def send_home(h, joined, level):
        z_out[128 * h:128 * h + 128, :] = joined.astype(BF16)
        lz_out[h] = level

        def go(i):
            s = 8 * h + rem(i + 4 * h, 8)

            @pl.when(s != 4)
            def _():
                to = along(s - 4, core)
                at = rem(20 - s, 16)
                remote(z_part(z_out, s), z_in.at[at], pair(zs), to).start()
                remote(lz_out.at[h], lz_in.at[at], pair(lzs), to).start()

        loop(0, 8, go)

    low = lax.broadcasted_iota(jnp.int32, (1, HEAD), 1) < 64

    def level_of(lower, lower_odd, upper, upper_odd):
        lower = pltpu.roll(lower, 64, 1) if lower_odd else lower
        upper = upper if upper_odd else pltpu.roll(upper, 64, 1)
        return jnp.where(low, lower, upper)

    def join_second():
        arrived(o_in.at[pl.ds(1, 3)], pair(os))
        arrived(l_in.at[pl.ds(1, 3)], pair(ls))

        def block(a, k):
            levels = [l_all[0, 0, a, k]] + [l_in[t, a, k] for t in range(1, 4)]
            level, shares = combine(levels)
            values = [o_all[0, 0, a, k]] + [o_in[t, a, k] for t in range(1, 4)]
            joined = weighted([expand(share) for share in shares], values).astype(BF16)
            lp_out[a, k] = level
            for m in range(2):
                sub = 2 * k + m
                p_out[sub, a] = joined[64 * m:64 * m + 64]

                @pl.when(sub > 0)
                def _():
                    to = first_peer(a, sub)
                    remote(p_out.at[sub, a], p_in.at[4 - sub, a], pair(ps), to).start()
                    remote(lp_out.at[a, k], lp_in.at[4 - sub, a], pair(lps), to).start()

        for a in range(2):
            loop(0, 2, lambda i, a=a: block(a, 1 - i))

    def join_first():
        arrived(p_in.at[pl.ds(1, 3)], pair(ps))
        arrived(lp_in.at[pl.ds(1, 3)], pair(lps))
        levels = [level_of(lp_out[0, 0], 0, lp_out[1, 0], 0)]
        levels += [level_of(lp_in[r, 0], r % 2, lp_in[r, 1], r % 2) for r in range(1, 4)]
        level, shares = combine(levels)
        values = [part.reshape(HEAD, HEAD) for part in [p_out[0]] + [p_in[r] for r in range(1, 4)]]
        send_home(0, weighted([expand(share) for share in shares], values), level)

    def join_plane():
        for a in range(2):
            ob_in[0, 64 * a:64 * a + 64, :] = o_all[1, 0, a, 0, 0:64, :]
            lb_in[0, a] = l_all[1, 0, a, 0]
        arrived(lb_in.at[pl.ds(1, 15)], pair(lbs))
        levels = [level_of(lb_in[n, 0], n % 2, lb_in[n, 1], (n // 4) % 2) for n in range(16)]
        top = levels[0]
        for level in levels[1:]:
            top = jnp.maximum(top, level)
        total = jnp.exp(levels[0] - top)
        for level in levels[1:]:
            total = total + jnp.exp(level - top)
        whole = top + jnp.log(total)
        for n in range(16):
            share_b[n] = jnp.exp(levels[n] - whole)
        arrived(ob_in.at[pl.ds(1, 15)], pair(obs))

        def add(i, acc):
            for m in range(4):
                acc = acc + expand(share_b[4 * i + m]) * ob_in[4 * i + m].astype(F32)
            return acc

        send_home(1, lax.fori_loop(0, 4, add, jnp.zeros((HEAD, HEAD), F32)), whole)

    join_second()
    join_first()
    join_plane()
    sent(q_own.at[1], pair(swap))
    sent(q_z.at[pl.ds(0, 128)], pair(s1))
    sent(z_rows(9, 7), pair(s2))
    sent(k_all.at[pl.ds(1, 7)], (kv.at[0], kv.at[1]))
    sent(v_all.at[pl.ds(1, 7), :, pl.ds(0, HEAD)], (kv.at[2], kv.at[3]))
    for h in range(2):
        sent(q_all.at[h, 0, :, pl.ds(1, 3)], (s3.at[h], s3.at[h]))
        sent(q_all.at[h, pl.ds(1, 3)], (q4s.at[h], q4r.at[h, 0]))
    sent(o_in.at[pl.ds(1, 3)], pair(os))
    sent(l_in.at[pl.ds(1, 3)], pair(ls))
    sent(p_in.at[pl.ds(1, 3)], pair(ps))
    sent(lp_in.at[pl.ds(1, 3)], pair(lps))
    sent(ob_in.at[pl.ds(1, 15)], pair(obs))
    sent(lb_in.at[pl.ds(1, 15)], pair(lbs))
    z_in[0] = z_out[64:80, :]
    lz_in[0] = lz_out[0]
    arrived(z_in.at[pl.ds(1, 15)], pair(zs))
    arrived(lz_in.at[pl.ds(1, 15)], pair(lzs))
    lane16 = lax.broadcasted_iota(jnp.int32, (16, HEAD), 1) - lax.broadcasted_iota(jnp.int32, (16, HEAD), 0)

    def join_z(w):
        levels, values = [], []
        for m in range(4):
            at = w + 4 * m
            offset = rem(20 - at, 8) * 16
            wide = jnp.broadcast_to(lz_in[at], (16, HEAD))
            levels.append(jnp.sum(jnp.where(lane16 == offset, wide, 0.0), axis=1, keepdims=True))
            values.append(z_in[at])
        _, shares = combine(levels)
        joined = weighted(shares, values)
        f_in[w] = joined[:8]
        s_out[w] = joined[8:]

    loop(0, 4, join_z)
    remote(s_out, s_in, pair(fs), other).start()

    def give(w, c, heads):
        for g in range(4):
            at = pl.multiple_of((4 * (2 * rem(u + w, 4) + c) + g) * HEAD, HEAD)
            out_ref[:, pl.ds(at, HEAD)] = heads[w, 2 * g:2 * g + 2, :].astype(BF16)

    loop(0, 4, lambda w: give(w, core, f_in))
    arrived(s_in, pair(fs))
    loop(0, 4, lambda w: give(w, 1 - core, s_in))
    sent(z_in.at[pl.ds(1, 15)], pair(zs))
    sent(lz_in.at[pl.ds(1, 15)], pair(lzs))
    sent(s_in, pair(fs))


def per_device(queries, keys, values, window_blocks):
    dma = pltpu.SemaphoreType.DMA
    vmem = pltpu.VMEM
    return pl.pallas_call(
        kernel,
        out_shape=jax.ShapeDtypeStruct(queries.shape, BF16),
        in_specs=[pl.BlockSpec(memory_space=pl.ANY)] * 4,
        out_specs=pl.BlockSpec(memory_space=pltpu.VMEM),
        scratch_shapes=[
            pltpu.SMEM((16,), jnp.int32),
            vmem((2, 2, 4096), BF16), vmem((4, 16, HEAD), F32), vmem((4, 16, HEAD), BF16), vmem((256, HEAD), BF16),
            vmem((2, 4, 2, 4, 64, HEAD), BF16), vmem((8, HEAD, HEAD), BF16), vmem((8, HEAD, 2 * HEAD), BF16),
            vmem((32, HEAD), F32), vmem((32, HEAD, HEAD), F32), vmem((8, HEAD), F32),
            vmem((2, 4, 2, 2, HEAD, HEAD), BF16), vmem((2, 4, 2, 2, 1, HEAD), F32),
            vmem((4, 2, 2, HEAD, HEAD), BF16), vmem((4, 2, 2, 1, HEAD), F32),
            vmem((4, 2, 64, HEAD), BF16), vmem((2, 2, 1, HEAD), F32),
            vmem((4, 2, 64, HEAD), BF16), vmem((4, 2, 1, HEAD), F32),
            vmem((16, HEAD, HEAD), BF16), vmem((16, 2, 1, HEAD), F32), vmem((16, 1, HEAD), F32),
            vmem((256, HEAD), BF16), vmem((2, 1, HEAD), F32),
            vmem((16, 16, HEAD), BF16), vmem((16, 1, HEAD), F32),
            vmem((4, 8, HEAD), F32), vmem((4, 8, HEAD), F32), vmem((4, 8, HEAD), F32),
            dma((4,)), dma((2,)), dma((2,)), dma((2,)), dma((2,)), dma((2, 2, 4)), dma((2,)), dma((2, 4)), dma((4,)),
            dma((2,)), dma((2,)), dma((2,)), dma((2,)), dma((2,)), dma((2,)), dma((2,)), dma((2,)), dma((2,)),
        ],
        compiler_params=pltpu.CompilerParams(
            collective_id=0, has_side_effects=True, vmem_limit_bytes=58 * 1024 * 1024
        ),
    )(queries, keys, values, window_blocks)


def solution(mesh):
    return jax.shard_map(
        per_device,
        mesh=mesh,
        in_specs=(
            P(("row", "col", "uly"), None),
            P(("col", "row", "uly"), None),
            P(("col", "row", "uly"), None),
            P(),
        ),
        out_specs=P(("row", "col", "uly"), None),
        check_vma=False,
    )
```

```python
import math

import jax
import jax.numpy as jnp
from jax import lax
from jax.experimental import pallas as pl
from jax.experimental.pallas import tpu as pltpu
from jax.sharding import PartitionSpec as P

HEAD = 128
MESH = pl.DeviceIdType.MESH
SCALE = 1.0 / math.sqrt(HEAD)
HIDDEN = -1e30
F32, BF16 = jnp.float32, jnp.bfloat16


def expand(row):
    return jnp.transpose(jnp.broadcast_to(row, (HEAD, HEAD)))


def combine(levels):
    top = jnp.maximum(jnp.maximum(levels[0], levels[1]), jnp.maximum(levels[2], levels[3]))
    shares = [jnp.exp(level - top) for level in levels]
    total = (shares[0] + shares[1]) + (shares[2] + shares[3])
    inverse = 1.0 / total
    return top + jnp.log(total), [share * inverse for share in shares]


def weighted(shares, values):
    acc = shares[0] * values[0].astype(F32)
    for share, value in zip(shares[1:], values[1:]):
        acc = acc + share * value.astype(F32)
    return acc


def kernel(
    q_ref, k_ref, v_ref, wb_ref, out_ref,
    wb, q_own, q_f32, q_cls, q_z, q_all, k_all, v_all, pos, thr, key_pos,
    o_all, l_all, o_in, l_in, p_out, lp_out, p_in, lp_in, ob_in, lb_in, share_b,
    z_out, lz_out, z_in, lz_in, s_out, s_in, f_in,
    own, swap, s1, s2, s3, s3r, q4s, q4r, kv, os, ls, ps, lps, obs, lbs, zs, lzs, fs,
):
    u = lax.axis_index("uly")
    row = lax.axis_index("row")
    col = lax.axis_index("col")
    rem, div = lax.rem, lax.div
    x, core = div(row, 2), rem(row, 2)
    y, z_high = rem(col, 4), div(col, 4)
    z = z_high * 4 + u

    def along(d, core_at):
        z_at = rem(z + (d + 16), 16)
        return {"uly": rem(z_at, 4), "row": 2 * x + core_at, "col": div(z_at, 4) * 4 + y}

    def plane(dx, dy):
        return {"uly": u, "row": 2 * rem(x + dx, 4) + core, "col": 4 * z_high + rem(y + dy, 4)}

    def remote(src, dst, sems, to):
        return pltpu.make_async_remote_copy(
            src_ref=src, dst_ref=dst, send_sem=sems[0], recv_sem=sems[1], device_id=to, device_id_type=MESH
        )

    other = {"uly": u, "row": 2 * x + 1 - core, "col": col}

    def pair(sem):
        return sem.at[0], sem.at[1]

    def arrived(ref, sems):
        remote(ref, ref, sems, other).wait_recv()

    def sent(ref, sems):
        remote(ref, ref, sems, other).wait_send()

    def loop(start, stop, body):
        def step(i, carry):
            body(i)
            return carry

        lax.fori_loop(start, stop, step, 0)

    d2 = 2 - 4 * core
    barrier = pltpu.get_barrier_semaphore()

    def greet(to):
        pl.semaphore_signal(barrier, inc=1, device_id=to, device_id_type=MESH)

    for d in (4, -4, 3, -3, 2, -2):
        greet(along(d, core))
    greet(plane(2, 0))
    greet(plane(0, 2))
    greet(along(d2, 1 - core))
    for d in (1, -1):
        greet(along(d, 1 - core))
        greet(along(d, core))
        greet(plane(d + 4, 0))
        greet(plane(0, d + 4))
    greet(other)
    own_q = pltpu.make_async_copy(q_ref, q_own.at[0], own.at[0])
    own_q.start()
    own_wb = pltpu.make_async_copy(wb_ref, wb, own.at[1])
    own_wb.start()

    def features(ref, group):
        return ref.at[:, pl.ds(pl.multiple_of(group * HEAD, HEAD), HEAD)]

    def v_place(slot):
        return v_all.at[slot]

    my_group = 2 * u + core
    own_k = pltpu.make_async_copy(features(k_ref, my_group), k_all.at[0], own.at[2])
    own_v = pltpu.make_async_copy(features(v_ref, my_group), v_place(0), own.at[3])
    own_k.start()
    own_v.start()
    pl.semaphore_wait(barrier, 18)

    remote(q_ref, q_own.at[1], pair(swap), other).start()
    own_q.wait()
    own_wb.wait()
    arrived(q_own.at[1], pair(swap))

    def pack(c):
        for r in range(2):
            for g in range(4):
                at = pl.multiple_of(((2 * c + core) * 4 + g) * HEAD, HEAD)
                q_f32[c, 8 * r + 2 * g:8 * r + 2 * g + 2, :] = q_own[r, :, pl.ds(at, HEAD)].astype(F32)
        q_cls[c] = q_f32[c].astype(BF16)

    loop(0, 4, pack)

    def z_rows(at, n):
        return q_z.at[pl.ds(pl.multiple_of(16 * at, 16), 16 * n)]

    for d in (4, -4, 3, -3, 2, -2, 1, -1):
        remote(q_cls.at[rem(u + d + 4, 4)], z_rows(4 - d, 1), pair(s1), along(d, core)).start()
    q_z[64:80, :] = q_cls[u]

    def spread(what):
        def one(group, slot, to):
            src = features(v_ref if what else k_ref, group)
            dst = v_place(slot) if what else k_all.at[slot]
            remote(src, dst, (kv.at[2 * what], kv.at[2 * what + 1]), to).start()

        for d, slot in ((d2, 6 + core), (1, 2 + core), (-1, 4 + core)):
            for c in range(2):
                one(2 * rem(u + d + 4, 4) + c, slot, along(d, c))
        one(2 * u + 1 - core, 1, other)

    spread(0)

    blk = lax.broadcasted_iota(jnp.int32, (32, HEAD), 0)
    lane = lax.broadcasted_iota(jnp.int32, (32, HEAD), 1)
    half, step, side, sub = blk >> 4, (blk >> 2) & 3, (blk >> 1) & 1, 2 * (blk & 1) + (lane >> 6)
    ys = (y + jnp.where(side == 0, step, sub)) & 3
    xs = (x + jnp.where(side == 0, sub, step)) & 3
    cs = jnp.where((lane & 8) == 0, core, 1 - core)
    z_src = (z + 8 * half + 4 * side + ((lane >> 4) & 3) + 12) & 15
    which = 2 * (2 * xs + cs) + (z_src >> 3)
    block_at = jnp.zeros((32, HEAD), jnp.int32)
    for i in range(16):
        block_at = jnp.where(which == i, wb[i], block_at)
    within = (((z_src >> 2) & 1) * 4 + ys) * 8 + (z_src & 3) * 2 + (lane & 1)
    pos[...] = (64 * block_at + within).astype(F32)
    lane_f = lax.broadcasted_iota(jnp.int32, (1, HEAD), 1).astype(F32)
    sources = [(z, core), (z, 1 - core), (z - 1, 0), (z - 1, 1), (z + 1, 0), (z + 1, 1), (z - 2, 0), (z + 2, 1)]
    for j, (zt, c) in enumerate(sources):
        zt = rem(zt + 16, 16)
        base = div(zt, 4) * 16384 + y * 4096 + x * 1024 + c * 512 + rem(zt, 4) * 128
        key_pos[j:j + 1, :] = lane_f + base.astype(F32)

    def spread_pos(b):
        thr[b] = expand(pos[pl.ds(b, 1), :])

    def first_peer(a, i):
        return plane(0, i) if a else plane(i, 0)

    def second_peer(a, i):
        return plane(i, 0) if a else plane(0, i)

    def first(h):
        for a in range(2):
            mine = q_z.at[pl.ds(128 * h + 64 * a, 64)]

            def go(i):
                remote(mine, q_all.at[h, 0, a, 4 - i], (s3.at[h], s3r.at[h, a, 4 - i]), first_peer(a, i)).start()

            loop(1, 4, go)
        for a in range(2):
            mine = q_z.at[pl.ds(128 * h + 64 * a, 64)]

            def go_on(i):
                remote(mine, q_all.at[h, 4 - i, a, 0], (q4s.at[h], q4r.at[h, 4 - i]), second_peer(a, i)).start()

            loop(1, 4, go_on)
            q_all[h, 0, a, 0] = q_z[128 * h + 64 * a:128 * h + 64 * a + 64, :]

    def second(h):
        def pass_on(j):
            r = j + div(j, 2) - 2 * div(j, 3)
            for a in range(2):
                block = q_all.at[h, 0, a, r]
                arrived(block, (s3.at[h], s3r.at[h, a, r]))

                def go(i):
                    remote(block, q_all.at[h, 4 - i, a, r], (q4s.at[h], q4r.at[h, 4 - i]), second_peer(a, i)).start()

                loop(1, 4, go)

        loop(1, 4, pass_on)

    arrived(q_z.at[pl.ds(0, 128)], pair(s1))
    remote(z_rows(5, 4), z_rows(9, 4), pair(s2), along(-4, core)).start()
    remote(z_rows(1, 3), z_rows(13, 3), pair(s2), along(4, core)).start()
    first(0)

    spread(1)
    loop(0, 32, spread_pos)
    second(0)
    arrived(z_rows(9, 7), pair(s2))
    first(1)

    own_k.wait()
    own_v.wait()
    arrived(k_all.at[pl.ds(1, 7)], (kv.at[0], kv.at[1]))
    arrived(v_all.at[pl.ds(1, 7)], (kv.at[2], kv.at[3]))

    eye = lax.broadcasted_iota(jnp.int32, (HEAD, HEAD), 0) == lax.broadcasted_iota(jnp.int32, (HEAD, HEAD), 1)

    def chunk(i):
        h, t = div(i, 4), rem(i, 4)

        pl.when(i == 7)(join_second)

        @pl.when(i == 1)
        def _():
            second(1)

        @pl.when(t > 0)
        def _():
            arrived(q_all.at[h, t], (q4s.at[h], q4r.at[h, t]))

        for a in range(2):
            q = q_all[h, t, a].reshape(256, HEAD)
            scores = lax.dot_general(
                q, k_all[...].reshape(1024, HEAD), (((1,), (1,)), ((), ())), preferred_element_type=F32
            )
            limit = thr[pl.ds(4 * i + 2 * a, 2)].reshape(256, HEAD)
            parts = [
                jnp.where(key_pos[j:j + 1, :] <= limit, scores[:, j * HEAD:(j + 1) * HEAD], HIDDEN) for j in range(8)
            ]
            top = parts[0]
            for part in parts[1:]:
                top = jnp.maximum(top, part)
            top = jnp.max(top, axis=1, keepdims=True) * SCALE
            parts = [jnp.exp(part * SCALE - top) for part in parts]
            total = (parts[0] + parts[1]) + (parts[2] + parts[3])
            total = total + ((parts[4] + parts[5]) + (parts[6] + parts[7]))
            total = jnp.sum(total, axis=1, keepdims=True)
            weights = jnp.concatenate([part.astype(BF16) for part in parts], axis=1)
            sums = lax.dot_general(
                weights, v_all[...].reshape(1024, HEAD), (((1,), (0,)), ((), ())), preferred_element_type=F32
            )
            o_all[h, t, a] = (sums / total).astype(BF16).reshape(2, HEAD, HEAD)
            level = top + jnp.log(total)
            for r in range(2):
                l_all[h, t, a, r] = jnp.sum(
                    jnp.where(eye, level[r * HEAD:(r + 1) * HEAD], 0.0), axis=0, keepdims=True
                )

        @pl.when((t > 0) & (h == 0))
        def _():
            for a in range(2):
                to = second_peer(a, t)
                remote(o_all.at[0, t, a], o_in.at[4 - t, a], pair(os), to).start()
                remote(l_all.at[0, t, a], l_in.at[4 - t, a], pair(ls), to).start()

        @pl.when(h == 1)
        def _():
            for a in range(2):
                for sub in range(4):

                    @pl.when((t > 0) | (sub > 0))
                    def _():
                        back_t, back_sub = rem(4 - t, 4), (4 - sub) % 4
                        to = plane(t, sub) if a else plane(sub, t)
                        there = 4 * back_sub + back_t if a else 4 * back_t + back_sub
                        part = o_all.at[1, t, a, sub // 2, pl.ds(64 * (sub % 2), 64)]
                        remote(part, ob_in.at[there, pl.ds(64 * a, 64)], pair(obs), to).start()
                        remote(l_all.at[1, t, a, sub // 2], lb_in.at[there, a], pair(lbs), to).start()

    def z_part(ref, s):
        return ref.at[pl.ds(pl.multiple_of(16 * s, 16), 16)]

    def send_home(h, joined, level):
        z_out[128 * h:128 * h + 128, :] = joined.astype(BF16)
        lz_out[h] = level

        def go(i):
            s = 8 * h + rem(i + 4 * h, 8)

            @pl.when(s != 4)
            def _():
                to = along(s - 4, core)
                at = rem(20 - s, 16)
                remote(z_part(z_out, s), z_in.at[at], pair(zs), to).start()
                remote(lz_out.at[h], lz_in.at[at], pair(lzs), to).start()

        loop(0, 8, go)

    low = lax.broadcasted_iota(jnp.int32, (1, HEAD), 1) < 64

    def level_of(lower, lower_odd, upper, upper_odd):
        lower = pltpu.roll(lower, 64, 1) if lower_odd else lower
        upper = upper if upper_odd else pltpu.roll(upper, 64, 1)
        return jnp.where(low, lower, upper)

    def join_second():
        arrived(o_in.at[pl.ds(1, 3)], pair(os))
        arrived(l_in.at[pl.ds(1, 3)], pair(ls))

        def block(a, k):
            levels = [l_all[0, 0, a, k]] + [l_in[t, a, k] for t in range(1, 4)]
            level, shares = combine(levels)
            values = [o_all[0, 0, a, k]] + [o_in[t, a, k] for t in range(1, 4)]
            joined = weighted([expand(share) for share in shares], values).astype(BF16)
            lp_out[a, k] = level
            for m in range(2):
                sub = 2 * k + m
                p_out[sub, a] = joined[64 * m:64 * m + 64]

                @pl.when(sub > 0)
                def _():
                    to = first_peer(a, sub)
                    remote(p_out.at[sub, a], p_in.at[4 - sub, a], pair(ps), to).start()
                    remote(lp_out.at[a, k], lp_in.at[4 - sub, a], pair(lps), to).start()

        for a in range(2):
            loop(0, 2, lambda i, a=a: block(a, 1 - i))

    def join_first():
        arrived(p_in.at[pl.ds(1, 3)], pair(ps))
        arrived(lp_in.at[pl.ds(1, 3)], pair(lps))
        levels = [level_of(lp_out[0, 0], 0, lp_out[1, 0], 0)]
        levels += [level_of(lp_in[r, 0], r % 2, lp_in[r, 1], r % 2) for r in range(1, 4)]
        level, shares = combine(levels)
        values = [part.reshape(HEAD, HEAD) for part in [p_out[0]] + [p_in[r] for r in range(1, 4)]]
        send_home(0, weighted([expand(share) for share in shares], values), level)

    def join_plane():
        for a in range(2):
            ob_in[0, 64 * a:64 * a + 64, :] = o_all[1, 0, a, 0, 0:64, :]
            lb_in[0, a] = l_all[1, 0, a, 0]
        arrived(lb_in.at[pl.ds(1, 15)], pair(lbs))
        levels = [level_of(lb_in[n, 0], n % 2, lb_in[n, 1], (n // 4) % 2) for n in range(16)]
        top = levels[0]
        for level in levels[1:]:
            top = jnp.maximum(top, level)
        total = jnp.exp(levels[0] - top)
        for level in levels[1:]:
            total = total + jnp.exp(level - top)
        whole = top + jnp.log(total)
        for n in range(16):
            share_b[n] = jnp.exp(levels[n] - whole)
        arrived(ob_in.at[pl.ds(1, 15)], pair(obs))

        def add(i, acc):
            for m in range(4):
                acc = acc + expand(share_b[4 * i + m]) * ob_in[4 * i + m].astype(F32)
            return acc

        send_home(1, lax.fori_loop(0, 4, add, jnp.zeros((HEAD, HEAD), F32)), whole)

    loop(0, 8, chunk)
    join_first()
    join_plane()
    sent(q_own.at[1], pair(swap))
    sent(q_z.at[pl.ds(0, 128)], pair(s1))
    sent(z_rows(9, 7), pair(s2))
    sent(k_all.at[pl.ds(1, 7)], (kv.at[0], kv.at[1]))
    sent(v_all.at[pl.ds(1, 7)], (kv.at[2], kv.at[3]))
    for h in range(2):
        sent(q_all.at[h, 0, :, pl.ds(1, 3)], (s3.at[h], s3.at[h]))
        sent(q_all.at[h, pl.ds(1, 3)], (q4s.at[h], q4r.at[h, 0]))
    sent(o_in.at[pl.ds(1, 3)], pair(os))
    sent(l_in.at[pl.ds(1, 3)], pair(ls))
    sent(p_in.at[pl.ds(1, 3)], pair(ps))
    sent(lp_in.at[pl.ds(1, 3)], pair(lps))
    sent(ob_in.at[pl.ds(1, 15)], pair(obs))
    sent(lb_in.at[pl.ds(1, 15)], pair(lbs))
    z_in[0] = z_out[64:80, :]
    lz_in[0] = lz_out[0]
    arrived(z_in.at[pl.ds(1, 15)], pair(zs))
    arrived(lz_in.at[pl.ds(1, 15)], pair(lzs))
    lane16 = lax.broadcasted_iota(jnp.int32, (16, HEAD), 1) - lax.broadcasted_iota(jnp.int32, (16, HEAD), 0)

    def join_z(w):
        levels, values = [], []
        for m in range(4):
            at = w + 4 * m
            offset = rem(20 - at, 8) * 16
            wide = jnp.broadcast_to(lz_in[at], (16, HEAD))
            levels.append(jnp.sum(jnp.where(lane16 == offset, wide, 0.0), axis=1, keepdims=True))
            values.append(z_in[at])
        _, shares = combine(levels)
        joined = weighted(shares, values)
        f_in[w] = joined[:8]
        s_out[w] = joined[8:]

    loop(0, 4, join_z)
    remote(s_out, s_in, pair(fs), other).start()

    def give(w, c, heads):
        for g in range(4):
            at = pl.multiple_of((4 * (2 * rem(u + w, 4) + c) + g) * HEAD, HEAD)
            out_ref[:, pl.ds(at, HEAD)] = heads[w, 2 * g:2 * g + 2, :].astype(BF16)

    loop(0, 4, lambda w: give(w, core, f_in))
    arrived(s_in, pair(fs))
    loop(0, 4, lambda w: give(w, 1 - core, s_in))
    sent(z_in.at[pl.ds(1, 15)], pair(zs))
    sent(lz_in.at[pl.ds(1, 15)], pair(lzs))
    sent(s_in, pair(fs))


def per_device(queries, keys, values, window_blocks):
    dma = pltpu.SemaphoreType.DMA
    vmem = pltpu.VMEM
    return pl.pallas_call(
        kernel,
        out_shape=jax.ShapeDtypeStruct(queries.shape, BF16),
        in_specs=[pl.BlockSpec(memory_space=pl.ANY)] * 4,
        out_specs=pl.BlockSpec(memory_space=pltpu.VMEM),
        scratch_shapes=[
            pltpu.SMEM((16,), jnp.int32),
            vmem((2, 2, 4096), BF16), vmem((4, 16, HEAD), F32), vmem((4, 16, HEAD), BF16), vmem((256, HEAD), BF16),
            vmem((2, 4, 2, 4, 64, HEAD), BF16), vmem((8, HEAD, HEAD), BF16), vmem((8, HEAD, HEAD), BF16),
            vmem((32, HEAD), F32), vmem((32, HEAD, HEAD), F32), vmem((8, HEAD), F32),
            vmem((2, 4, 2, 2, HEAD, HEAD), BF16), vmem((2, 4, 2, 2, 1, HEAD), F32),
            vmem((4, 2, 2, HEAD, HEAD), BF16), vmem((4, 2, 2, 1, HEAD), F32),
            vmem((4, 2, 64, HEAD), BF16), vmem((2, 2, 1, HEAD), F32),
            vmem((4, 2, 64, HEAD), BF16), vmem((4, 2, 1, HEAD), F32),
            vmem((16, HEAD, HEAD), BF16), vmem((16, 2, 1, HEAD), F32), vmem((16, 1, HEAD), F32),
            vmem((256, HEAD), BF16), vmem((2, 1, HEAD), F32),
            vmem((16, 16, HEAD), BF16), vmem((16, 1, HEAD), F32),
            vmem((4, 8, HEAD), F32), vmem((4, 8, HEAD), F32), vmem((4, 8, HEAD), F32),
            dma((4,)), dma((2,)), dma((2,)), dma((2,)), dma((2,)), dma((2, 2, 4)), dma((2,)), dma((2, 4)), dma((4,)),
            dma((2,)), dma((2,)), dma((2,)), dma((2,)), dma((2,)), dma((2,)), dma((2,)), dma((2,)), dma((2,)),
        ],
        compiler_params=pltpu.CompilerParams(
            collective_id=0, has_side_effects=True, vmem_limit_bytes=58 * 1024 * 1024
        ),
    )(queries, keys, values, window_blocks)


def solution(mesh):
    return jax.shard_map(
        per_device,
        mesh=mesh,
        in_specs=(
            P(("row", "col", "uly"), None),
            P(("col", "row", "uly"), None),
            P(("col", "row", "uly"), None),
            P(),
        ),
        out_specs=P(("row", "col", "uly"), None),
        check_vma=False,
    )
```
